512 devices in a mesh: ctx: 64 (over x, y_lo, z), width: 8 (over y_hi, core).
Axes of the slice: x: 4, y: 8 (y_hi: 4, y_lo: 2; y = y_hi * 2 + y_lo), z: 8, core: 2. Of those that a mesh axis runs over, the one named last changes fastest.
Arguments:
- queries: bfloat16 [512, 32768], P('width', 'ctx'), may hold values from -6 to 6
- keys: bfloat16 [512, 32768], P('width', 'ctx'), may hold values from -6 to 6
- values: bfloat16 [512, 32768], P('width', 'ctx'), may hold values from -6 to 6
- cotangent: bfloat16 [512, 32768], P('width', 'ctx'), may hold values from -6 to 6
- filters: float32 [32, 32768], P('width', 'ctx'), may hold values from -1.05 to 1.05
Outputs:
- mixed: bfloat16 [512, 32768], P('width', 'ctx')
- query_grad: bfloat16 [512, 32768], P('width', 'ctx')
- key_grad: bfloat16 [512, 32768], P('width', 'ctx')
- value_grad: bfloat16 [512, 32768], P('width', 'ctx')
- filter_grad: bfloat16 [32, 32768], P('width', 'ctx')
The draws below stay inside these ranges and needn't reach their ends.
All inputs are finite; a program needn't handle non-finite values.
Results may differ from the reference program's by a relative error of at most 0.018.
Values may be sent and summed in bfloat16 or wider, within the bound.
No kernel may reach another device: no remote copies, remote signals or barrier semaphores. Data moves between devices by JAX's collectives and lax.ppermute only.
A program may use at most 64 MiB of HBM per device.

```python
import math
import jax
import jax.numpy as jnp
from jax import lax

CHANNELS = 512
GROUP = 16
FILTERS = 32
LENGTH = 32768
SPAN = 65536
FIRST = 512
SECOND = 128


def draw_filters(key, part):
    key = jax.random.fold_in(key, 11)
    rate_key, kind_key, tap_key = jax.random.split(key, 3)
    position = jnp.arange(LENGTH, dtype=jnp.float32)[None, :]
    unit_draw = jax.random.uniform(rate_key, (FILTERS, 1), jnp.float32)
    kind_draw = jax.random.uniform(kind_key, (FILTERS, 1), jnp.float32)
    slow_rate = 0.05 / LENGTH * jnp.exp(unit_draw * math.log(40.0))
    fast_rate = 1.0 / (30.0 + 20.0 * unit_draw)
    decay_rate = jnp.where(kind_draw < 0.35, fast_rate, slow_rate)
    raw_taps = jax.random.truncated_normal(tap_key, -4.0, 4.0, (FILTERS, LENGTH), jnp.float32)
    return raw_taps * jnp.sqrt(2.0 * decay_rate) * jnp.exp(-decay_rate * position)


def block_levels(key, extent, pieces, low, largest):
    factor_of, own = 1.0, jax.random.fold_in(key, 6)
    for dim, parts in pieces:
        heights = jnp.exp(jax.random.uniform(jax.random.fold_in(own, dim), (parts,), jnp.float32, low / len(pieces), largest / len(pieces)))
        factor_of = factor_of * jnp.repeat(heights, extent[dim] // parts).reshape([-1 if axis == dim else 1 for axis in range(len(extent))])
    return factor_of


def gaussian(stream_key, dims, scale, bound, pieces=(), kind=jnp.bfloat16):
    loudness = block_levels(stream_key, dims, pieces, -0.22, 0.18) if pieces else 1.0
    values = jax.random.normal(stream_key, dims, jnp.float32) * scale * loudness
    return jnp.minimum(jnp.maximum(values, -bound), bound).astype(kind)


def setup_inputs(seed: int = 0) -> dict:
    key_list = jax.random.split(jax.random.key(seed), 6)
    queries = gaussian(key_list[0], (CHANNELS, LENGTH), 1.0, 6.0, ((0, 8), (1, 64)))
    keys = gaussian(key_list[1], (CHANNELS, LENGTH), 1.0, 6.0, ((0, 8), (1, 64)))
    values = gaussian(key_list[2], (CHANNELS, LENGTH), 1.0, 6.0, ((0, 8), (1, 64)))
    cotangent = gaussian(key_list[3], (CHANNELS, LENGTH), 1.0, 6.0, ((0, 8), (1, 64)))
    filters = draw_filters(jax.random.fold_in(key_list[5], 71), 0)
    return dict(queries=queries, keys=keys, values=values, cotangent=cotangent, filters=filters)


exact_mode = lax.Precision.HIGHEST

def angles(count_rows, count_cols, period, row_start):
    row_ids = row_start + jnp.arange(count_rows, dtype=jnp.int32)[:, None]
    col_ids = jnp.arange(count_cols, dtype=jnp.int32)[None, :]
    return (row_ids * col_ids % period).astype(jnp.float32) * (2.0 * math.pi / period)

def first_table(half_rows, period):
    grid = angles(half_rows, period, period, 0)
    cosine_part, sine_part = (jnp.cos(grid), jnp.sin(grid))
    return jnp.stack([jnp.concatenate([cosine_part, -sine_part], 1), jnp.concatenate([sine_part, cosine_part], 1)]).astype(jnp.bfloat16)

def second_table(order_len):
    grid = angles(order_len, order_len, order_len, 0)
    cosine_part, sine_part = (jnp.cos(grid), jnp.sin(grid))
    return jnp.stack([jnp.concatenate([cosine_part, -sine_part], 1), jnp.concatenate([sine_part, cosine_part], 1)], axis=1).astype(jnp.bfloat16)

def back_table(order_len):
    grid = angles(order_len, order_len, order_len, 0)
    cosine_part, sine_part = (jnp.cos(grid), jnp.sin(grid))
    return jnp.concatenate([jnp.concatenate([cosine_part, sine_part], 1), jnp.concatenate([-sine_part, cosine_part], 1)], 0).astype(jnp.bfloat16)

def last_table(period, half_rows):
    grid = angles(period, half_rows, period, 0)
    cosine_part, sine_part = (jnp.cos(grid), jnp.sin(grid))
    return jnp.stack([jnp.stack([cosine_part, sine_part], 1), jnp.stack([-sine_part, cosine_part], 1)], 1).astype(jnp.bfloat16)

def turn_forward(mixed, angle_grid):
    col_count = angle_grid.shape[1]
    real_part, imag_part = (mixed[..., :col_count], mixed[..., col_count:])
    cosine_part, sine_part = (jnp.cos(angle_grid), jnp.sin(angle_grid))
    return jnp.stack([real_part * cosine_part + imag_part * sine_part, imag_part * cosine_part - real_part * sine_part], axis=-2).astype(jnp.bfloat16)

def turn_back(opened, angle_grid):
    col_count = angle_grid.shape[1]
    real_part, imag_part = (opened[..., :col_count], opened[..., col_count:])
    cosine_part, sine_part = (jnp.cos(angle_grid), jnp.sin(angle_grid))
    return jnp.stack([real_part * cosine_part - imag_part * sine_part, imag_part * cosine_part + real_part * sine_part], axis=-2).astype(jnp.bfloat16)

def halves(spectrum):
    wide = lax.optimization_barrier(spectrum).astype(jnp.float32)
    return (wide[..., :FIRST], wide[..., FIRST:])

def forward(signal, tables, twist_fwd):
    signal_count, width_in = (signal.shape[0], signal.shape[1])
    row_blocks = signal.reshape(signal_count, width_in, LENGTH // FIRST, FIRST).astype(jnp.float32)
    mixed = jnp.einsum('srba,rbo->sao', row_blocks, tables[0][:width_in].astype(jnp.float32), precision=exact_mode)
    turned = lax.optimization_barrier(turn_forward(mixed, twist_fwd)).astype(jnp.float32)
    return jnp.einsum('sprk,prq->skq', turned, tables[1].astype(jnp.float32), precision=exact_mode).astype(jnp.bfloat16)

def inverse(spectrum, width_out, scale_out, tables, twist_back):
    wide = lax.optimization_barrier(spectrum).astype(jnp.float32)
    opened = jnp.einsum('skx,xo->sko', wide, tables[2].astype(jnp.float32), precision=exact_mode)
    turned = lax.optimization_barrier(turn_back(opened, twist_back)).astype(jnp.float32)
    row_blocks = jnp.einsum('sqra,qrxh->sxha', turned, tables[3][:, :, :width_out].astype(jnp.float32), precision=exact_mode)
    result = lax.optimization_barrier((row_blocks * scale_out).astype(jnp.bfloat16))
    return result.reshape(spectrum.shape[0], width_out, LENGTH)

def reference(queries, keys, values, cotangent, filters):
    half_rows = LENGTH // FIRST
    tables = (first_table(half_rows, SECOND), second_table(FIRST), back_table(FIRST), last_table(SECOND, half_rows))
    twist_fwd = angles(FIRST, SECOND, SPAN, 0)
    twist_back = angles(SECOND, FIRST, SPAN, 0)
    plain_scale = 1.0 / SPAN
    root_scale = 1.0 / math.sqrt(GROUP * LENGTH)
    product = (keys.astype(jnp.float32) * values.astype(jnp.float32)).astype(jnp.bfloat16)
    gated = (cotangent.astype(jnp.float32) * queries.astype(jnp.float32)).astype(jnp.bfloat16)
    taps = filters.astype(jnp.bfloat16)
    pair_count = CHANNELS // (2 * FILTERS)

    def split(array):
        return array.reshape(pair_count, 2, FILTERS, LENGTH).transpose(2, 0, 1, 3)

    def merge(array):
        return array.transpose(1, 2, 0, 3).reshape(CHANNELS, LENGTH)

    def one_filter(inputs):
        prod_sig, grad_sig, query_sig, cot_sig, key_sig, value_sig, tap_sig = inputs
        prod_spec = forward(prod_sig, tables, twist_fwd)
        grad_spec = forward(grad_sig, tables, twist_fwd)
        taps_spec = forward(tap_sig.reshape(1, 1, LENGTH), tables, twist_fwd)
        taps_real, taps_imag = halves(taps_spec)
        prod_real, prod_imag = halves(prod_spec)
        grad_real, grad_imag = halves(grad_spec)
        resp_spec = jnp.concatenate([taps_real * prod_real - taps_imag * prod_imag, taps_real * prod_imag + taps_imag * prod_real], -1).astype(jnp.bfloat16)
        pull_spec = jnp.concatenate([taps_real * grad_real + taps_imag * grad_imag, taps_real * grad_imag - taps_imag * grad_real], -1).astype(jnp.bfloat16)
        lag_sum = jnp.concatenate([lax.optimization_barrier(jnp.sum(grad_real * prod_real + grad_imag * prod_imag, 0, keepdims=True)), lax.optimization_barrier(jnp.sum(grad_imag * prod_real - grad_real * prod_imag, 0, keepdims=True))], -1)
        lag_spec = (lag_sum * root_scale).astype(jnp.bfloat16)
        response = inverse(resp_spec, 2, plain_scale, tables, twist_back).astype(jnp.float32)
        pulled = inverse(pull_spec, 2, plain_scale, tables, twist_back).astype(jnp.float32)
        lagged = inverse(lag_spec, 1, plain_scale, tables, twist_back)
        mixed = (query_sig.astype(jnp.float32) * response).astype(jnp.bfloat16)
        query_grad = (cot_sig.astype(jnp.float32) * response).astype(jnp.bfloat16)
        key_grad = (pulled * value_sig.astype(jnp.float32)).astype(jnp.bfloat16)
        value_grad = (pulled * key_sig.astype(jnp.float32)).astype(jnp.bfloat16)
        return (mixed, query_grad, key_grad, value_grad, lagged[0, 0])
    results = lax.map(one_filter, (split(product), split(gated), split(queries), split(cotangent), split(keys), split(values), taps))
    return (merge(results[0]), merge(results[1]), merge(results[2]), merge(results[3]), results[4])
```

```python
import functools
import math

import jax
import jax.numpy as jnp
import ml_dtypes
import numpy as np
from jax import lax
from jax.experimental import pallas as pl
from jax.experimental.pallas import tpu as pltpu
from jax.sharding import PartitionSpec as P

GROUP = 16
LENGTH = 32768
SPAN = 65536
LANES = 128
COLS = 512
ROWS = LENGTH // LANES
CTX = 64
SUB = 4
AXES = ("ctx", "width")


def grid_angles(rows, cols, period):
    grid = np.outer(np.arange(rows), np.arange(cols)) % period
    return grid * (2.0 * math.pi / period)


def tables():
    def low(array):
        return np.asarray(array, dtype=np.float32).astype(ml_dtypes.bfloat16)

    grid = grid_angles(COLS, ROWS, COLS)
    first = low(np.concatenate([np.cos(grid), -np.sin(grid)], 0))
    last = low(np.concatenate([np.cos(grid.T), -np.sin(grid.T)], 1))
    grid = grid_angles(LANES, LANES, LANES)
    cosine, sine = np.cos(grid), np.sin(grid)
    second = low(np.block([[cosine, -sine], [sine, cosine]]))
    back = low(np.block([[cosine, sine], [-sine, cosine]]))
    grid = grid_angles(COLS, LANES, SPAN)
    twist = np.concatenate([np.cos(grid), np.sin(grid)], 1).astype(np.float32)
    return first, second, back, last, twist


def dot(left, right):
    return jnp.dot(left, right, preferred_element_type=jnp.float32)


def low(array):
    return array.astype(jnp.bfloat16)


def wide(array):
    return array.astype(jnp.float32)


def rows_of(piece):
    pairs = piece.reshape(CTX // 2, 2, SUB, piece.shape[-1])
    joined = jnp.concatenate([pairs[:, 0], pairs[:, 1]], axis=1)
    return joined.reshape(CTX * SUB, piece.shape[-1])


def pieces_of(rows):
    return rows.reshape(rows.shape[0] // SUB, SUB, rows.shape[1])


def turn(real, imag, twist, sign):
    cosine, sine = twist[:, :LANES], twist[:, LANES:]
    if sign < 0:
        return real * cosine + imag * sine, imag * cosine - real * sine
    return real * cosine - imag * sine, imag * cosine + real * sine


def spectrum(opened, twist, second):
    real, imag = turn(opened[:COLS], opened[COLS:], twist, -1)
    return dot(low(jnp.concatenate([real, imag], 1)), second)


def unturned(real, imag, back, twist):
    opened = dot(low(jnp.concatenate([real, imag], 1)), back)
    return turn(opened[:, :LANES], opened[:, LANES:], twist, 1)


def pack_kernel(keys, values, cotangent, queries, filters, out, prods, grads, taps):
    width = lax.axis_index("width")
    prod = wide(keys[...]) * wide(values[...])
    grad = wide(cotangent[...]) * wide(queries[...])
    for s in range(SUB):
        lanes = slice(LANES * s, LANES * (s + 1))
        prods[pl.ds(s, CTX, stride=SUB), :] = prod[:, lanes]
        grads[pl.ds(s, CTX, stride=SUB), :] = grad[:, lanes]
        taps[pl.ds(s, SUB, stride=SUB), :] = filters[:, lanes]
    own = taps[...]
    for block in range(8):
        for half in range(2):
            rows = pl.ds(16 * block + 128 * half, 16)
            piece = jnp.concatenate([prods[rows, :], grads[rows, :], own], 1)
            place = 8 * jnp.bitwise_xor(width, block) + 4 * half
            out[pl.ds(place, 4)] = low(pieces_of(piece))


def spread_kernel(arrived, first, second, back, last, twist, prod_out, grad_out, lag_out):
    pair = rows_of(wide(arrived[:, :, : 2 * LANES]))
    opened = dot(first[...], low(pair))
    turns = twist[...]
    prod = spectrum(opened[:, :LANES], turns, second[...])
    grad = spectrum(opened[:, LANES:], turns, second[...])
    prod_out[...] = low(prod)
    grad_out[...] = low(grad)
    prod_real, prod_imag = prod[:, :LANES], prod[:, LANES:]
    grad_real, grad_imag = grad[:, :LANES], grad[:, LANES:]
    real, imag = unturned(
        grad_real * prod_real + grad_imag * prod_imag,
        grad_imag * prod_real - grad_real * prod_imag,
        back[...],
        turns,
    )
    lag = dot(last[...], low(jnp.concatenate([real, imag], 0)))
    lag = lag * (1.0 / (SPAN * math.sqrt(GROUP * LENGTH)))
    lag_out[...] = low(pieces_of(lag))


def filter_kernel(arrived, prod, grad, first, second, back, last, twist, out):
    turns = twist[...]
    opened = dot(first[...], low(rows_of(wide(arrived[...]))))
    taps = spectrum(opened, turns, second[...])
    taps_real, taps_imag = taps[:, :LANES], taps[:, LANES:]
    prod_real, prod_imag = wide(prod[:, :LANES]), wide(prod[:, LANES:])
    grad_real, grad_imag = wide(grad[:, :LANES]), wide(grad[:, LANES:])
    real = taps_real * (prod_real - grad_imag) - taps_imag * (prod_imag - grad_real)
    imag = taps_real * (prod_imag + grad_real) + taps_imag * (prod_real + grad_imag)
    real, imag = unturned(real, imag, back[...], turns)
    real, imag = low(real), low(imag)
    stacked = jnp.concatenate(
        [jnp.concatenate([real, imag], 1), jnp.concatenate([imag, -real], 1)], 0
    )
    both = dot(last[...], stacked) * (1.0 / SPAN)
    out[...] = low(pieces_of(both))


def gate_kernel(
    arrived, keys, values, cotangent, queries, mixed, query_grad, key_grad, value_grad, filter_grad, resps, pulls
):
    width = lax.axis_index("width")
    for block in range(8):
        for half in range(2):
            place = 8 * jnp.bitwise_xor(width, block) + 4 * half
            piece = wide(arrived[pl.ds(place, 4), :, : 2 * LANES]).reshape(16, 2 * LANES)
            rows = pl.ds(16 * block + 128 * half, 16)
            resps[rows, :] = piece[:, :LANES]
            pulls[rows, :] = piece[:, LANES:]
    lag = wide(arrived[:, :, 2 * LANES :]).reshape(GROUP, SUB, SUB, LANES)
    lag = jnp.sum(lag, 0)
    for s in range(SUB):
        lanes = slice(LANES * s, LANES * (s + 1))
        response = resps[pl.ds(s, CTX, stride=SUB), :]
        pulled = pulls[pl.ds(s, CTX, stride=SUB), :]
        mixed[:, lanes] = low(wide(queries[:, lanes]) * response)
        query_grad[:, lanes] = low(wide(cotangent[:, lanes]) * response)
        key_grad[:, lanes] = low(pulled * wide(values[:, lanes]))
        value_grad[:, lanes] = low(pulled * wide(keys[:, lanes]))
        filter_grad[:, lanes] = low(lag[:, s, :])


def shape(*dims):
    return jax.ShapeDtypeStruct(dims, jnp.bfloat16)


def call(kernel, out_shape, scratch=(), flops=0, **kwargs):
    return pl.pallas_call(
        kernel,
        out_shape=out_shape,
        scratch_shapes=scratch,
        cost_estimate=pl.CostEstimate(flops=flops, bytes_accessed=1 << 20, transcendentals=0),
        compiler_params=pltpu.CompilerParams(vmem_limit_bytes=24 << 20),
        **kwargs,
    )


def on_device(first, second, back, last, twist, queries, keys, values, cotangent, filters):
    pairs = [
        (c * 8 + w, c * 8 + (w ^ (c // 8))) for c in range(CTX) for w in range(8)
    ]
    channels, local = queries.shape
    packed = call(
        pack_kernel,
        shape(CTX, SUB, 3 * LANES),
        (
            pltpu.VMEM((channels * SUB, LANES), jnp.float32),
            pltpu.VMEM((channels * SUB, LANES), jnp.float32),
            pltpu.VMEM((SUB * SUB, LANES), jnp.float32),
        ),
    )(keys, values, cotangent, queries, filters)
    arrived = lax.all_to_all(packed, "ctx", split_axis=0, concat_axis=0, tiled=True)
    taps = lax.ppermute(arrived[:, :, 2 * LANES :], AXES, pairs)
    prod, grad, lag = call(
        spread_kernel,
        (shape(COLS, 2 * LANES), shape(COLS, 2 * LANES), shape(CTX, SUB, LANES)),
        flops=400_000_000,
    )(arrived, first, second, back, last, twist)
    lag = lax.ppermute(lag, AXES, pairs)
    both = call(
        filter_kernel, shape(CTX, SUB, 2 * LANES), flops=340_000_000
    )(taps, prod, grad, first, second, back, last, twist)
    outgoing = jnp.concatenate([both, lag], -1)
    returned = lax.all_to_all(outgoing, "ctx", split_axis=0, concat_axis=0, tiled=True)
    full = shape(channels, local)
    return call(
        gate_kernel,
        (full, full, full, full, shape(SUB, local)),
        (pltpu.VMEM((channels * SUB, LANES), jnp.float32),) * 2,
    )(returned, keys, values, cotangent, queries)


def solution(mesh):
    spec = P("width", "ctx")
    fixed = tables()
    mapped = jax.shard_map(
        on_device,
        mesh=mesh,
        in_specs=(P(),) * len(fixed) + (spec,) * 5,
        out_specs=(spec,) * 5,
        check_vma=False,
    )

    def run(queries, keys, values, cotangent, filters):
        return mapped(*fixed, queries, keys, values, cotangent, filters)

    return run
```

```python
import math

import jax
import jax.numpy as jnp
import ml_dtypes
import numpy as np
from jax import lax
from jax.experimental import pallas as pl
from jax.experimental.pallas import tpu as pltpu
from jax.sharding import PartitionSpec as P

GROUP = 16
LENGTH = 32768
SPAN = 65536
LANES = 128
COLS = 512
ROWS = LENGTH // LANES
CTX = 64
SUB = 4
AXES = ("ctx", "width")


def grid_angles(rows, cols, period):
    grid = np.outer(np.arange(rows), np.arange(cols)) % period
    return grid * (2.0 * math.pi / period)


def tables():
    def low(array):
        return np.asarray(array, dtype=np.float32).astype(ml_dtypes.bfloat16)

    grid = grid_angles(COLS, ROWS, COLS)
    first = low(np.concatenate([np.cos(grid), -np.sin(grid)], 0))
    last = low(np.concatenate([np.cos(grid.T), -np.sin(grid.T)], 1))
    grid = grid_angles(LANES, LANES, LANES)
    cosine, sine = np.cos(grid), np.sin(grid)
    second = low(np.block([[cosine, -sine], [sine, cosine]]))
    back = low(np.block([[cosine, sine], [-sine, cosine]]))
    grid = grid_angles(COLS, LANES, SPAN)
    twist = np.concatenate([np.cos(grid), np.sin(grid)], 1).astype(np.float32)
    return first, second, back, last, twist


def dot(left, right):
    return jnp.dot(left, right, preferred_element_type=jnp.float32)


def low(array):
    return array.astype(jnp.bfloat16)


def wide(array):
    return array.astype(jnp.float32)


def rows_of(piece):
    pairs = piece.reshape(CTX // 2, 2, SUB, piece.shape[-1])
    joined = jnp.concatenate([pairs[:, 0], pairs[:, 1]], axis=1)
    return joined.reshape(CTX * SUB, piece.shape[-1])


def pieces_of(rows):
    return rows.reshape(rows.shape[0] // SUB, SUB, rows.shape[1])


def turn(real, imag, twist, sign):
    cosine, sine = twist[:, :LANES], twist[:, LANES:]
    if sign < 0:
        return real * cosine + imag * sine, imag * cosine - real * sine
    return real * cosine - imag * sine, imag * cosine + real * sine


def spectrum(opened, twist, second):
    real, imag = turn(opened[:COLS], opened[COLS:], twist, -1)
    return dot(low(jnp.concatenate([real, imag], 1)), second)


def unturned(real, imag, back, twist):
    opened = dot(low(jnp.concatenate([real, imag], 1)), back)
    return turn(opened[:, :LANES], opened[:, LANES:], twist, 1)


def stretch(width, block, half):
    turn_by = jnp.bitwise_xor(width, block)
    odd, high, core = (turn_by // 2) % 2, turn_by // 4, turn_by % 2
    mixed = 1 - jnp.bitwise_xor((width // 2) % 2, high)
    outer = odd * half + (1 - odd) * mixed
    low_y = odd * high + (1 - odd) * half
    return 32 * outer + 16 * odd + 8 * low_y + 4 * core


def partner(c, w):
    outer, odd, low_y, core = c // 32, (c // 16) % 2, (c // 8) % 2, (c // 4) % 2
    if odd:
        high = low_y
    else:
        high = int((w // 2) % 2 == outer)
    other = c ^ 8 if high and not odd else c
    return other * 8 + (w ^ (4 * high + 2 * odd + core))


def fetch(sources, targets, sems):
    copies = [
        pltpu.make_async_copy(source, target, sems.at[i])
        for i, (source, target) in enumerate(zip(sources, targets))
    ]
    for copy in copies:
        copy.start()
    for copy in copies:
        copy.wait()


def keep_kernel(*refs):
    count = (len(refs) - 2) // 2
    fetch(refs[1 : count + 1], refs[count + 1 : -1], refs[-1])


def pack_kernel(*refs):
    sources, out, kept, (prods, grads, taps, sems) = refs[:5], refs[5], refs[6:11], refs[11:]
    fetch(sources, kept, sems)
    keys, values, cotangent, queries, filters = kept
    width = lax.axis_index("width")
    prod = wide(keys[...]) * wide(values[...])
    grad = wide(cotangent[...]) * wide(queries[...])
    for s in range(SUB):
        lanes = slice(LANES * s, LANES * (s + 1))
        prods[pl.ds(s, CTX, stride=SUB), :] = prod[:, lanes]
        grads[pl.ds(s, CTX, stride=SUB), :] = grad[:, lanes]
        taps[pl.ds(s, SUB, stride=SUB), :] = filters[:, lanes]
    own = taps[...]
    for block in range(8):
        for half in range(2):
            rows = pl.ds(16 * block + 128 * half, 16)
            piece = jnp.concatenate([prods[rows, :], grads[rows, :], own], 1)
            out[pl.ds(stretch(width, block, half), 4)] = low(pieces_of(piece))


def spread_kernel(arrived, first, second, back, last, twist, prod_out, grad_out, crossing):
    pair = rows_of(wide(arrived[:, :, : 2 * LANES]))
    opened = dot(first[...], low(pair))
    turns = twist[...]
    prod = spectrum(opened[:, :LANES], turns, second[...])
    grad = spectrum(opened[:, LANES:], turns, second[...])
    prod_out[...] = low(prod)
    grad_out[...] = low(grad)
    prod_real, prod_imag = prod[:, :LANES], prod[:, LANES:]
    grad_real, grad_imag = grad[:, :LANES], grad[:, LANES:]
    real, imag = unturned(
        grad_real * prod_real + grad_imag * prod_imag,
        grad_imag * prod_real - grad_real * prod_imag,
        back[...],
        turns,
    )
    lag = dot(last[...], low(jnp.concatenate([real, imag], 0)))
    lag = lag * (1.0 / (SPAN * math.sqrt(GROUP * LENGTH)))
    crossing[:, :, :LANES] = arrived[:, :, 2 * LANES :]
    crossing[:, :, LANES:] = low(pieces_of(lag))


def filter_kernel(crossed, prod, grad, first, second, back, last, twist, out):
    turns = twist[...]
    opened = dot(first[...], low(rows_of(wide(crossed[:, :, :LANES]))))
    taps = spectrum(opened, turns, second[...])
    taps_real, taps_imag = taps[:, :LANES], taps[:, LANES:]
    prod_real, prod_imag = wide(prod[:, :LANES]), wide(prod[:, LANES:])
    grad_real, grad_imag = wide(grad[:, :LANES]), wide(grad[:, LANES:])
    real = taps_real * (prod_real - grad_imag) - taps_imag * (prod_imag - grad_real)
    imag = taps_real * (prod_imag + grad_real) + taps_imag * (prod_real + grad_imag)
    real, imag = unturned(real, imag, back[...], turns)
    real, imag = low(real), low(imag)
    stacked = jnp.concatenate(
        [jnp.concatenate([real, imag], 1), jnp.concatenate([imag, -real], 1)], 0
    )
    both = dot(last[...], stacked) * (1.0 / SPAN)
    out[:, :, : 2 * LANES] = low(pieces_of(both))
    out[:, :, 2 * LANES :] = crossed[:, :, LANES:]


def gate_kernel(
    arrived, keys, values, cotangent, queries, mixed, query_grad, key_grad, value_grad, filter_grad, resps, pulls
):
    width = lax.axis_index("width")
    for block in range(8):
        for half in range(2):
            place = stretch(width, block, half)
            piece = wide(arrived[pl.ds(place, 4), :, : 2 * LANES]).reshape(16, 2 * LANES)
            rows = pl.ds(16 * block + 128 * half, 16)
            resps[rows, :] = piece[:, :LANES]
            pulls[rows, :] = piece[:, LANES:]
    lag = wide(arrived[:, :, 2 * LANES :]).reshape(GROUP, SUB, SUB, LANES)
    lag = jnp.sum(lag, 0)
    for s in range(SUB):
        lanes = slice(LANES * s, LANES * (s + 1))
        response = resps[pl.ds(s, CTX, stride=SUB), :]
        pulled = pulls[pl.ds(s, CTX, stride=SUB), :]
        mixed[:, lanes] = low(wide(queries[:, lanes]) * response)
        query_grad[:, lanes] = low(wide(cotangent[:, lanes]) * response)
        key_grad[:, lanes] = low(pulled * wide(values[:, lanes]))
        value_grad[:, lanes] = low(pulled * wide(keys[:, lanes]))
        filter_grad[:, lanes] = low(lag[:, s, :])


def shape(*dims):
    return jax.ShapeDtypeStruct(dims, jnp.bfloat16)


def call(kernel, out_shape, scratch=(), flops=0, room=24, **kwargs):
    return pl.pallas_call(
        kernel,
        out_shape=out_shape,
        scratch_shapes=scratch,
        cost_estimate=pl.CostEstimate(flops=flops, bytes_accessed=1 << 20, transcendentals=0),
        compiler_params=pltpu.CompilerParams(vmem_limit_bytes=room << 20),
        **kwargs,
    )


def on_device(first, second, back, last, twist, queries, keys, values, cotangent, filters):
    pairs = [(c * 8 + w, partner(c, w)) for c in range(CTX) for w in range(8)]
    channels, local = queries.shape
    def like(array, memory):
        return memory(array.shape, array.dtype)

    anywhere = pl.BlockSpec(memory_space=pl.ANY)
    sources = (keys, values, cotangent, queries, filters)
    packed = call(
        pack_kernel,
        shape(CTX, SUB, 3 * LANES),
        (
            *(like(x, pltpu.VMEM) for x in sources),
            pltpu.VMEM((channels * SUB, LANES), jnp.float32),
            pltpu.VMEM((channels * SUB, LANES), jnp.float32),
            pltpu.VMEM((SUB * SUB, LANES), jnp.float32),
            pltpu.SemaphoreType.DMA((len(sources),)),
        ),
        in_specs=[anywhere] * len(sources),
        room=57,
    )(*sources)
    arrived = lax.all_to_all(packed, "ctx", split_axis=0, concat_axis=0, tiled=True)
    sources = (first, second, back, last, twist, keys, values, cotangent, queries)
    kept = call(
        keep_kernel,
        tuple(like(x, jax.ShapeDtypeStruct) for x in sources),
        (pltpu.SemaphoreType.DMA((len(sources),)),),
        flops=1_000_000_000,
        in_specs=[anywhere] * (len(sources) + 1),
    )(packed, *sources)
    fixed, gates = kept[:5], kept[5:]
    prod, grad, crossing = call(
        spread_kernel,
        (shape(COLS, 2 * LANES), shape(COLS, 2 * LANES), shape(CTX, SUB, 2 * LANES)),
        flops=400_000_000,
    )(arrived, *fixed)
    crossed = lax.ppermute(crossing, AXES, pairs)
    outgoing = call(filter_kernel, shape(CTX, SUB, 3 * LANES), flops=340_000_000)(
        crossed, prod, grad, *fixed
    )
    returned = lax.all_to_all(outgoing, "ctx", split_axis=0, concat_axis=0, tiled=True)
    full = shape(channels, local)
    return call(
        gate_kernel,
        (full, full, full, full, shape(SUB, local)),
        (pltpu.VMEM((channels * SUB, LANES), jnp.float32),) * 2,
    )(returned, *gates)


def solution(mesh):
    spec = P("width", "ctx")
    fixed = tables()
    mapped = jax.shard_map(
        on_device,
        mesh=mesh,
        in_specs=(P(),) * len(fixed) + (spec,) * 5,
        out_specs=(spec,) * 5,
        check_vma=False,
    )

    def run(queries, keys, values, cotangent, filters):
        return mapped(*fixed, queries, keys, values, cotangent, filters)

    return run
```

```python
import math

import jax
import jax.numpy as jnp
import ml_dtypes
import numpy as np
from jax import lax
from jax.experimental import pallas as pl
from jax.experimental.pallas import tpu as pltpu
from jax.sharding import PartitionSpec as P

GROUP = 16
LENGTH = 32768
SPAN = 65536
LANES = 128
COLS = 512
ROWS = LENGTH // LANES
CTX = 64
SUB = 4
AXES = ("ctx", "width")


def grid_angles(rows, cols, period):
    grid = np.outer(np.arange(rows), np.arange(cols)) % period
    return grid * (2.0 * math.pi / period)


def tables():
    def low(array):
        return np.asarray(array, dtype=np.float32).astype(ml_dtypes.bfloat16)

    grid = grid_angles(COLS, ROWS, COLS)
    first = low(np.concatenate([np.cos(grid), -np.sin(grid)], 0))
    last = low(np.concatenate([np.cos(grid.T), -np.sin(grid.T)], 1))
    grid = grid_angles(LANES, LANES, LANES)
    cosine, sine = np.cos(grid), np.sin(grid)
    second = low(np.block([[cosine, -sine], [sine, cosine]]))
    back = low(np.block([[cosine, sine], [-sine, cosine]]))
    grid = grid_angles(COLS, LANES, SPAN)
    twist = np.concatenate([np.cos(grid), np.sin(grid)], 1).astype(np.float32)
    return first, second, back, last, twist


def dot(left, right):
    return jnp.dot(left, right, preferred_element_type=jnp.float32)


def low(array):
    return array.astype(jnp.bfloat16)


def wide(array):
    return array.astype(jnp.float32)


def rows_of(piece):
    pairs = piece.reshape(CTX // 2, 2, SUB, piece.shape[-1])
    joined = jnp.concatenate([pairs[:, 0], pairs[:, 1]], axis=1)
    return joined.reshape(CTX * SUB, piece.shape[-1])


def pieces_of(rows):
    return rows.reshape(rows.shape[0] // SUB, SUB, rows.shape[1])


def turn(real, imag, twist, sign):
    cosine, sine = twist[:, :LANES], twist[:, LANES:]
    if sign < 0:
        return real * cosine + imag * sine, imag * cosine - real * sine
    return real * cosine - imag * sine, imag * cosine + real * sine


def spectrum(opened, twist, second):
    real, imag = turn(opened[:COLS], opened[COLS:], twist, -1)
    return dot(low(jnp.concatenate([real, imag], 1)), second)


def unturned(real, imag, back, twist):
    opened = dot(low(jnp.concatenate([real, imag], 1)), back)
    return turn(opened[:, :LANES], opened[:, LANES:], twist, 1)


def stretch(width, block, half):
    turn_by = jnp.bitwise_xor(width, block)
    odd, high, core = (turn_by // 2) % 2, turn_by // 4, turn_by % 2
    mixed = 1 - jnp.bitwise_xor((width // 2) % 2, high)
    outer = odd * half + (1 - odd) * mixed
    low_y = odd * mixed + (1 - odd) * half
    return 32 * outer + 16 * core + 8 * low_y + 4 * (1 - odd)


def partner(c, w):
    outer, core, low_y, odd = c // 32, (c // 16) % 2, (c // 8) % 2, 1 - (c // 4) % 2
    high = int((w // 2) % 2 == (low_y if odd else outer))
    other = c ^ 8 if high or odd else c
    return other * 8 + (w ^ (4 * high + 2 * odd + core))


def fetch(sources, targets, sems):
    copies = [
        pltpu.make_async_copy(source, target, sems.at[i])
        for i, (source, target) in enumerate(zip(sources, targets))
    ]
    for copy in copies:
        copy.start()
    for copy in copies:
        copy.wait()


def keep_kernel(*refs):
    count = (len(refs) - 2) // 2
    fetch(refs[1 : count + 1], refs[count + 1 : -1], refs[-1])


def pack_kernel(*refs):
    sources, out, kept, (prods, grads, taps, sems) = refs[:5], refs[5], refs[6:11], refs[11:]
    fetch(sources, kept, sems)
    keys, values, cotangent, queries, filters = kept
    width = lax.axis_index("width")
    prod = wide(keys[...]) * wide(values[...])
    grad = wide(cotangent[...]) * wide(queries[...])
    for s in range(SUB):
        lanes = slice(LANES * s, LANES * (s + 1))
        prods[pl.ds(s, CTX, stride=SUB), :] = prod[:, lanes]
        grads[pl.ds(s, CTX, stride=SUB), :] = grad[:, lanes]
        taps[pl.ds(s, SUB, stride=SUB), :] = filters[:, lanes]
    own = taps[...]
    for block in range(8):
        for half in range(2):
            rows = pl.ds(16 * block + 128 * half, 16)
            piece = jnp.concatenate([prods[rows, :], grads[rows, :], own], 1)
            out[pl.ds(stretch(width, block, half), 4)] = low(pieces_of(piece))


def spread_kernel(arrived, first, second, back, last, twist, prod_out, grad_out, crossing):
    pair = rows_of(wide(arrived[:, :, : 2 * LANES]))
    opened = dot(first[...], low(pair))
    turns = twist[...]
    prod = spectrum(opened[:, :LANES], turns, second[...])
    grad = spectrum(opened[:, LANES:], turns, second[...])
    prod_out[...] = low(prod)
    grad_out[...] = low(grad)
    prod_real, prod_imag = prod[:, :LANES], prod[:, LANES:]
    grad_real, grad_imag = grad[:, :LANES], grad[:, LANES:]
    real, imag = unturned(
        grad_real * prod_real + grad_imag * prod_imag,
        grad_imag * prod_real - grad_real * prod_imag,
        back[...],
        turns,
    )
    lag = dot(last[...], low(jnp.concatenate([real, imag], 0)))
    lag = lag * (1.0 / (SPAN * math.sqrt(GROUP * LENGTH)))
    crossing[:, :, :LANES] = arrived[:, :, 2 * LANES :]
    crossing[:, :, LANES:] = low(pieces_of(lag))


def filter_kernel(crossed, prod, grad, first, second, back, last, twist, out):
    turns = twist[...]
    opened = dot(first[...], low(rows_of(wide(crossed[:, :, :LANES]))))
    taps = spectrum(opened, turns, second[...])
    taps_real, taps_imag = taps[:, :LANES], taps[:, LANES:]
    prod_real, prod_imag = wide(prod[:, :LANES]), wide(prod[:, LANES:])
    grad_real, grad_imag = wide(grad[:, :LANES]), wide(grad[:, LANES:])
    real = taps_real * (prod_real - grad_imag) - taps_imag * (prod_imag - grad_real)
    imag = taps_real * (prod_imag + grad_real) + taps_imag * (prod_real + grad_imag)
    real, imag = unturned(real, imag, back[...], turns)
    real, imag = low(real), low(imag)
    stacked = jnp.concatenate(
        [jnp.concatenate([real, imag], 1), jnp.concatenate([imag, -real], 1)], 0
    )
    both = dot(last[...], stacked) * (1.0 / SPAN)
    out[:, :, : 2 * LANES] = low(pieces_of(both))
    out[:, :, 2 * LANES :] = crossed[:, :, LANES:]


def gate_kernel(
    arrived, keys, values, cotangent, queries, mixed, query_grad, key_grad, value_grad, filter_grad, resps, pulls
):
    width = lax.axis_index("width")
    for block in range(8):
        for half in range(2):
            place = stretch(width, block, half)
            piece = wide(arrived[pl.ds(place, 4), :, : 2 * LANES]).reshape(16, 2 * LANES)
            rows = pl.ds(16 * block + 128 * half, 16)
            resps[rows, :] = piece[:, :LANES]
            pulls[rows, :] = piece[:, LANES:]
    lag = wide(arrived[:, :, 2 * LANES :]).reshape(GROUP, SUB, SUB, LANES)
    lag = jnp.sum(lag, 0)
    for s in range(SUB):
        lanes = slice(LANES * s, LANES * (s + 1))
        response = resps[pl.ds(s, CTX, stride=SUB), :]
        pulled = pulls[pl.ds(s, CTX, stride=SUB), :]
        mixed[:, lanes] = low(wide(queries[:, lanes]) * response)
        query_grad[:, lanes] = low(wide(cotangent[:, lanes]) * response)
        key_grad[:, lanes] = low(pulled * wide(values[:, lanes]))
        value_grad[:, lanes] = low(pulled * wide(keys[:, lanes]))
        filter_grad[:, lanes] = low(lag[:, s, :])


def shape(*dims):
    return jax.ShapeDtypeStruct(dims, jnp.bfloat16)


def call(kernel, out_shape, scratch=(), flops=0, room=24, **kwargs):
    return pl.pallas_call(
        kernel,
        out_shape=out_shape,
        scratch_shapes=scratch,
        cost_estimate=pl.CostEstimate(flops=flops, bytes_accessed=1 << 20, transcendentals=0),
        compiler_params=pltpu.CompilerParams(vmem_limit_bytes=room << 20),
        **kwargs,
    )


def on_device(first, second, back, last, twist, queries, keys, values, cotangent, filters):
    pairs = [(c * 8 + w, partner(c, w)) for c in range(CTX) for w in range(8)]
    channels, local = queries.shape
    def like(array, memory):
        return memory(array.shape, array.dtype)

    anywhere = pl.BlockSpec(memory_space=pl.ANY)
    sources = (keys, values, cotangent, queries, filters)
    packed = call(
        pack_kernel,
        shape(CTX, SUB, 3 * LANES),
        (
            *(like(x, pltpu.VMEM) for x in sources),
            pltpu.VMEM((channels * SUB, LANES), jnp.float32),
            pltpu.VMEM((channels * SUB, LANES), jnp.float32),
            pltpu.VMEM((SUB * SUB, LANES), jnp.float32),
            pltpu.SemaphoreType.DMA((len(sources),)),
        ),
        in_specs=[anywhere] * len(sources),
        room=57,
    )(*sources)
    arrived = lax.all_to_all(packed, "ctx", split_axis=0, concat_axis=0, tiled=True)
    sources = (first, second, back, last, twist, keys, values, cotangent, queries)
    kept = call(
        keep_kernel,
        tuple(like(x, jax.ShapeDtypeStruct) for x in sources),
        (pltpu.SemaphoreType.DMA((len(sources),)),),
        flops=1_000_000_000,
        in_specs=[anywhere] * (len(sources) + 1),
    )(packed, *sources)
    fixed, gates = kept[:5], kept[5:]
    prod, grad, crossing = call(
        spread_kernel,
        (shape(COLS, 2 * LANES), shape(COLS, 2 * LANES), shape(CTX, SUB, 2 * LANES)),
        flops=400_000_000,
    )(arrived, *fixed)
    crossed = lax.ppermute(crossing, AXES, pairs)
    outgoing = call(filter_kernel, shape(CTX, SUB, 3 * LANES), flops=340_000_000)(
        crossed, prod, grad, *fixed
    )
    returned = lax.all_to_all(outgoing, "ctx", split_axis=0, concat_axis=0, tiled=True)
    full = shape(channels, local)
    return call(
        gate_kernel,
        (full, full, full, full, shape(SUB, local)),
        (pltpu.VMEM((channels * SUB, LANES), jnp.float32),) * 2,
    )(returned, *gates)


def solution(mesh):
    spec = P("width", "ctx")
    fixed = tables()
    mapped = jax.shard_map(
        on_device,
        mesh=mesh,
        in_specs=(P(),) * len(fixed) + (spec,) * 5,
        out_specs=(spec,) * 5,
        check_vma=False,
    )

    def run(queries, keys, values, cotangent, filters):
        return mapped(*fixed, queries, keys, values, cotangent, filters)

    return run
```

```python
import math

import jax
import jax.numpy as jnp
import ml_dtypes
import numpy as np
from jax import lax
from jax.experimental import pallas as pl
from jax.experimental.pallas import tpu as pltpu
from jax.sharding import PartitionSpec as P

GROUP = 16
LENGTH = 32768
SPAN = 65536
LANES = 128
COLS = 512
ROWS = LENGTH // LANES
HALF = COLS // 2
EDGE = 16
KEPT = HALF + EDGE
CTX = 64
SUB = 4
AXES = ("ctx", "width")
ORDER_IN = np.random.RandomState(3).permutation(CTX).tolist()
ORDER_OUT = np.random.RandomState(2).permutation(CTX).tolist()


def grid_angles(rows, cols, period):
    grid = np.outer(np.arange(rows), np.arange(cols)) % period
    return grid * (2.0 * math.pi / period)


def tables():
    def low(array):
        return np.asarray(array, dtype=np.float32).astype(ml_dtypes.bfloat16)

    grid = grid_angles(HALF + 1, ROWS, COLS)
    first = np.concatenate([np.cos(grid[:HALF]), np.cos(grid[HALF:]), -np.sin(grid[1:HALF])], 0)
    weights = np.full((COLS, 1), 2.0)
    weights[[0, HALF]] = 1.0
    last = low((first * weights).T)
    grid = grid_angles(LANES, LANES, LANES)
    cosine, sine = np.cos(grid), np.sin(grid)
    second = low(np.block([[cosine, -sine], [sine, cosine]]))
    back = low(np.block([[cosine, sine], [-sine, cosine]]))
    grid = grid_angles(HALF + 1, LANES, SPAN)[np.minimum(np.arange(KEPT), HALF)]
    twist = np.concatenate([np.cos(grid), np.sin(grid)], 1).astype(np.float32)
    first, last = low(first)[:, row_order(ORDER_IN)], last[row_order(ORDER_OUT)]
    return first, second, back, last, twist


def dot(left, right):
    return jnp.dot(left, right, preferred_element_type=jnp.float32)


def low(array):
    return array.astype(jnp.bfloat16)


def wide(array):
    return array.astype(jnp.float32)


def rows_of(piece):
    pairs = piece.reshape(CTX // 2, 2, SUB, piece.shape[-1])
    joined = jnp.concatenate([pairs[:, 0], pairs[:, 1]], axis=1)
    return joined.reshape(CTX * SUB, piece.shape[-1])


def pieces_of(rows):
    return rows.reshape(rows.shape[0] // SUB, SUB, rows.shape[1])


def turn(real, imag, twist, sign):
    cosine, sine = twist[:, :LANES], twist[:, LANES:]
    if sign < 0:
        return real * cosine + imag * sine, imag * cosine - real * sine
    return real * cosine - imag * sine, imag * cosine + real * sine


def top_row(shape):
    return lax.broadcasted_iota(jnp.int32, shape, 0) == 0


def turned(opened, twist):
    real, imag = opened[:HALF], opened[HALF:]
    head = imag[:8]
    edge = jnp.broadcast_to(head[:1], (EDGE, LANES))
    head = jnp.where(top_row(head.shape), 0.0, head)
    real = jnp.concatenate([real, edge], 0)
    imag = jnp.concatenate([head, imag[8:], jnp.zeros_like(edge)], 0)
    real, imag = turn(real, imag, twist, -1)
    return low(jnp.concatenate([real, imag], 1))


def reopened(opened, twist):
    real, imag = turn(opened[:, :LANES], opened[:, LANES:], twist, 1)
    head = imag[:8]
    head = jnp.where(top_row(head.shape), real[HALF : HALF + 8], head)
    return low(jnp.concatenate([real[:HALF], head, imag[8:HALF]], 0))


def channel(c, w):
    outer, core, low_y, odd = c // 32, (c // 16) % 2, (c // 8) % 2, 1 - (c // 4) % 2
    high = int((w // 2) % 2 == (low_y if odd else outer))
    half = outer if odd else low_y
    return 4 * (w ^ (4 * high + 2 * odd + core)) + c % 4 + 32 * half


def packed_slots(order):
    words = [[0, 0] for _ in range(CTX)]
    for slot, c in enumerate(order):
        for w in range(8):
            words[channel(c, w)][w // 4] |= slot << (8 * (w % 4))
    return words


def slot_of(words, width):
    word = jnp.where(width < 4, jnp.int32(words[0]), jnp.int32(words[1]))
    return jnp.bitwise_and(jnp.right_shift(word, 8 * (width % 4)), 255)


def row_order(order):
    return [SUB * c + s for c in order for s in range(SUB)]


def partner(c, w):
    outer, core, low_y, odd = c // 32, (c // 16) % 2, (c // 8) % 2, 1 - (c // 4) % 2
    high = int((w // 2) % 2 == (low_y if odd else outer))
    other = c ^ 8 if high or odd else c
    return other * 8 + (w ^ (4 * high + 2 * odd + core))


def fetch(sources, targets, sems):
    copies = [
        pltpu.make_async_copy(source, target, sems.at[i])
        for i, (source, target) in enumerate(zip(sources, targets))
    ]
    for copy in copies:
        copy.start()
    for copy in copies:
        copy.wait()


def keep_kernel(*refs):
    count = (len(refs) - 2) // 2
    fetch(refs[1 : count + 1], refs[count + 1 : -1], refs[-1])


def pack_kernel(*refs):
    sources, out, kept, (prods, grads, taps, sems) = refs[:5], refs[5], refs[6:11], refs[11:]
    fetch(sources, kept, sems)
    keys, values, cotangent, queries, filters = kept
    width = lax.axis_index("width")
    prod = wide(keys[...]) * wide(values[...])
    grad = wide(cotangent[...]) * wide(queries[...])
    for s in range(SUB):
        lanes = slice(LANES * s, LANES * (s + 1))
        prods[pl.ds(s, CTX, stride=SUB), :] = prod[:, lanes]
        grads[pl.ds(s, CTX, stride=SUB), :] = grad[:, lanes]
        taps[pl.ds(s, SUB, stride=SUB), :] = filters[:, lanes]
    own = taps[...]
    words = packed_slots(ORDER_IN)
    for first in range(0, CTX, SUB):
        rows = pl.ds(SUB * first, SUB * SUB)
        pieces = jnp.concatenate([prods[rows, :], grads[rows, :], own], 1)
        pieces = low(pieces_of(pieces))
        for i in range(SUB):
            out[pl.ds(slot_of(words[first + i], width), 1)] = pieces[i : i + 1]


def spread_kernel(arrived, first, second, back, last, twist, spectra, crossing):
    pair = rows_of(wide(arrived[:, :, : 2 * LANES]))
    opened = dot(first[...], low(pair))
    turns = twist[...]
    both = [turned(opened[:, :LANES], turns), turned(opened[:, LANES:], turns)]
    both = dot(jnp.concatenate(both, 0), second[...])
    spectra[...] = low(both)
    prod_real, prod_imag = both[:KEPT, :LANES], both[:KEPT, LANES:]
    grad_real, grad_imag = both[KEPT:, :LANES], both[KEPT:, LANES:]
    real = grad_real * prod_real + grad_imag * prod_imag
    imag = grad_imag * prod_real - grad_real * prod_imag
    opened = dot(low(jnp.concatenate([real, imag], 1)), back[...])
    lag = dot(last[...], reopened(opened, turns))
    lag = lag * (1.0 / (SPAN * math.sqrt(GROUP * LENGTH)))
    crossing[:, :, :LANES] = arrived[:, :, 2 * LANES :]
    crossing[:, :, LANES:] = low(pieces_of(lag))


def filter_kernel(crossed, spectra, first, second, back, last, twist, out):
    turns = twist[...]
    opened = dot(first[...], low(rows_of(wide(crossed[:, :, :LANES]))))
    taps = dot(turned(opened, turns), second[...])
    taps_real, taps_imag = taps[:, :LANES], taps[:, LANES:]
    prod_real, prod_imag = wide(spectra[:KEPT, :LANES]), wide(spectra[:KEPT, LANES:])
    grad_real, grad_imag = wide(spectra[KEPT:, :LANES]), wide(spectra[KEPT:, LANES:])
    real = taps_real * prod_real - taps_imag * prod_imag
    imag = taps_real * prod_imag + taps_imag * prod_real
    response = jnp.concatenate([real, imag], 1)
    real = taps_real * grad_real + taps_imag * grad_imag
    imag = taps_real * grad_imag - taps_imag * grad_real
    pulled = jnp.concatenate([real, imag], 1)
    opened = dot(low(jnp.concatenate([response, pulled], 0)), back[...])
    pair = [reopened(opened[:KEPT], turns), reopened(opened[KEPT:], turns)]
    both = dot(last[...], jnp.concatenate(pair, 1)) * (1.0 / SPAN)
    out[:, :, : 2 * LANES] = low(pieces_of(both))
    out[:, :, 2 * LANES :] = crossed[:, :, LANES:]


def gate_kernel(
    arrived, keys, values, cotangent, queries, mixed, query_grad, key_grad, value_grad, filter_grad, resps, pulls
):
    width = lax.axis_index("width")
    words = packed_slots(ORDER_OUT)
    for first in range(0, CTX, SUB):
        pieces = [arrived[pl.ds(slot_of(words[first + i], width), 1)] for i in range(SUB)]
        pieces = wide(jnp.concatenate(pieces, 0)[:, :, : 2 * LANES]).reshape(SUB * SUB, 2 * LANES)
        rows = pl.ds(SUB * first, SUB * SUB)
        resps[rows, :] = pieces[:, :LANES]
        pulls[rows, :] = pieces[:, LANES:]
    lag = wide(arrived[:, :, 2 * LANES :])
    lag = [sum(lag[k] for k in range(CTX) if ORDER_OUT[k] % SUB == i) for i in range(SUB)]
    for s in range(SUB):
        lanes = slice(LANES * s, LANES * (s + 1))
        response = resps[pl.ds(s, CTX, stride=SUB), :]
        pulled = pulls[pl.ds(s, CTX, stride=SUB), :]
        mixed[:, lanes] = low(wide(queries[:, lanes]) * response)
        query_grad[:, lanes] = low(wide(cotangent[:, lanes]) * response)
        key_grad[:, lanes] = low(pulled * wide(values[:, lanes]))
        value_grad[:, lanes] = low(pulled * wide(keys[:, lanes]))
        filter_grad[:, lanes] = low(jnp.concatenate([part[s : s + 1] for part in lag], 0))


def shape(*dims):
    return jax.ShapeDtypeStruct(dims, jnp.bfloat16)


def call(kernel, out_shape, scratch=(), flops=0, room=24, **kwargs):
    return pl.pallas_call(
        kernel,
        out_shape=out_shape,
        scratch_shapes=scratch,
        cost_estimate=pl.CostEstimate(flops=flops, bytes_accessed=1 << 20, transcendentals=0),
        compiler_params=pltpu.CompilerParams(vmem_limit_bytes=room << 20),
        **kwargs,
    )


def exchange(pieces, order):
    return lax.all_to_all(
        pieces, "ctx", split_axis=0, concat_axis=0, axis_index_groups=[order], tiled=True
    )


def on_device(first, second, back, last, twist, queries, keys, values, cotangent, filters):
    pairs = [(c * 8 + w, partner(c, w)) for c in range(CTX) for w in range(8)]
    channels, local = queries.shape
    def like(array, memory):
        return memory(array.shape, array.dtype)

    anywhere = pl.BlockSpec(memory_space=pl.ANY)
    sources = (keys, values, cotangent, queries, filters)
    packed = call(
        pack_kernel,
        shape(CTX, SUB, 3 * LANES),
        (
            *(like(x, pltpu.VMEM) for x in sources),
            pltpu.VMEM((channels * SUB, LANES), jnp.float32),
            pltpu.VMEM((channels * SUB, LANES), jnp.float32),
            pltpu.VMEM((SUB * SUB, LANES), jnp.float32),
            pltpu.SemaphoreType.DMA((len(sources),)),
        ),
        in_specs=[anywhere] * len(sources),
        room=57,
    )(*sources)
    arrived = exchange(packed, ORDER_IN)
    sources = (first, second, back, last, twist, keys, values, cotangent, queries)
    kept = call(
        keep_kernel,
        tuple(like(x, jax.ShapeDtypeStruct) for x in sources),
        (pltpu.SemaphoreType.DMA((len(sources),)),),
        flops=1_000_000_000,
        in_specs=[anywhere] * (len(sources) + 1),
    )(packed, *sources)
    fixed, gates = kept[:5], kept[5:]
    spectra, crossing = call(
        spread_kernel,
        (shape(2 * KEPT, 2 * LANES), shape(CTX, SUB, 2 * LANES)),
        flops=250_000_000,
    )(arrived, *fixed)
    crossed = lax.ppermute(crossing, AXES, pairs)
    outgoing = call(filter_kernel, shape(CTX, SUB, 3 * LANES), flops=250_000_000)(
        crossed, spectra, *fixed
    )
    returned = exchange(outgoing, ORDER_OUT)
    full = shape(channels, local)
    return call(
        gate_kernel,
        (full, full, full, full, shape(SUB, local)),
        (pltpu.VMEM((channels * SUB, LANES), jnp.float32),) * 2,
    )(returned, *gates)


def solution(mesh):
    spec = P("width", "ctx")
    fixed = tables()
    mapped = jax.shard_map(
        on_device,
        mesh=mesh,
        in_specs=(P(),) * len(fixed) + (spec,) * 5,
        out_specs=(spec,) * 5,
        check_vma=False,
    )

    def run(queries, keys, values, cotangent, filters):
        return mapped(*fixed, queries, keys, values, cotangent, filters)

    return run
```

```python
import math

import jax
import jax.numpy as jnp
import ml_dtypes
import numpy as np
from jax import lax
from jax.experimental import pallas as pl
from jax.experimental.pallas import tpu as pltpu
from jax.sharding import PartitionSpec as P

GROUP = 16
LENGTH = 32768
SPAN = 65536
LANES = 128
COLS = 512
ROWS = LENGTH // LANES
HALF = COLS // 2
EDGE = 16
KEPT = HALF + EDGE
CTX = 64
SUB = 4
AXES = ("ctx", "width")


def shuffled(seed, start):
    order = np.random.RandomState(seed).permutation(CTX).tolist()
    at = order.index(start)
    return order[at:] + order[:at]


ORDER_IN = shuffled(3, 36)
ORDER_OUT = shuffled(9, 36)


def grid_angles(rows, cols, period):
    grid = np.outer(np.arange(rows), np.arange(cols)) % period
    return grid * (2.0 * math.pi / period)


def tables():
    def low(array):
        return np.asarray(array, dtype=np.float32).astype(ml_dtypes.bfloat16)

    grid = grid_angles(HALF + 1, ROWS, COLS)
    first = np.concatenate([np.cos(grid[:HALF]), np.cos(grid[HALF:]), -np.sin(grid[1:HALF])], 0)
    weights = np.full((COLS, 1), 2.0)
    weights[[0, HALF]] = 1.0
    last = low((first * weights).T)
    grid = grid_angles(LANES, LANES, LANES)
    cosine, sine = np.cos(grid), np.sin(grid)
    second = low(np.block([[cosine, -sine], [sine, cosine]]))
    back = low(np.block([[cosine, sine], [-sine, cosine]]))
    grid = grid_angles(HALF + 1, LANES, SPAN)[np.minimum(np.arange(KEPT), HALF)]
    twist = np.concatenate([np.cos(grid), np.sin(grid)], 1).astype(np.float32)
    first, last = low(first)[:, row_order(ORDER_IN)], last[row_order(ORDER_OUT)]
    return first, second, back, last, twist


def dot(left, right):
    return jnp.dot(left, right, preferred_element_type=jnp.float32)


def low(array):
    return array.astype(jnp.bfloat16)


def wide(array):
    return array.astype(jnp.float32)


def rows_of(piece):
    pairs = piece.reshape(CTX // 2, 2, SUB, piece.shape[-1])
    joined = jnp.concatenate([pairs[:, 0], pairs[:, 1]], axis=1)
    return joined.reshape(CTX * SUB, piece.shape[-1])


def pieces_of(rows):
    return rows.reshape(rows.shape[0] // SUB, SUB, rows.shape[1])


def turn(real, imag, twist, sign):
    cosine, sine = twist[:, :LANES], twist[:, LANES:]
    if sign < 0:
        return real * cosine + imag * sine, imag * cosine - real * sine
    return real * cosine - imag * sine, imag * cosine + real * sine


def top_row(shape):
    return lax.broadcasted_iota(jnp.int32, shape, 0) == 0


def turned(opened, twist):
    real, imag = opened[:HALF], opened[HALF:]
    head = imag[:8]
    edge = jnp.broadcast_to(head[:1], (EDGE, LANES))
    head = jnp.where(top_row(head.shape), 0.0, head)
    real = jnp.concatenate([real, edge], 0)
    imag = jnp.concatenate([head, imag[8:], jnp.zeros_like(edge)], 0)
    real, imag = turn(real, imag, twist, -1)
    return low(jnp.concatenate([real, imag], 1))


def reopened(opened, twist):
    real, imag = turn(opened[:, :LANES], opened[:, LANES:], twist, 1)
    head = imag[:8]
    head = jnp.where(top_row(head.shape), real[HALF : HALF + 8], head)
    return low(jnp.concatenate([real[:HALF], head, imag[8:HALF]], 0))


def channel(c, w):
    outer, core, low_y, odd = c // 32, (c // 16) % 2, (c // 8) % 2, 1 - (c // 4) % 2
    high = int((w // 2) % 2 == (low_y if odd else outer))
    half = outer if odd else low_y
    return 4 * (w ^ (4 * high + 2 * odd + core)) + c % 4 + 32 * half


def packed_slots(order):
    words = [[0, 0] for _ in range(CTX)]
    for slot, c in enumerate(order):
        for w in range(8):
            words[channel(c, w)][w // 4] |= slot << (8 * (w % 4))
    return words


def slot_of(words, width):
    word = jnp.where(width < 4, jnp.int32(words[0]), jnp.int32(words[1]))
    return jnp.bitwise_and(jnp.right_shift(word, 8 * (width % 4)), 255)


def row_order(order):
    return [SUB * c + s for c in order for s in range(SUB)]


def partner(c, w):
    outer, core, low_y, odd = c // 32, (c // 16) % 2, (c // 8) % 2, 1 - (c // 4) % 2
    high = int((w // 2) % 2 == (low_y if odd else outer))
    other = c ^ 8 if high or odd else c
    return other * 8 + (w ^ (4 * high + 2 * odd + core))


def fetch(sources, targets, sems):
    copies = [
        pltpu.make_async_copy(source, target, sems.at[i])
        for i, (source, target) in enumerate(zip(sources, targets))
    ]
    for copy in copies:
        copy.start()
    for copy in copies:
        copy.wait()


def keep_kernel(*refs):
    count = (len(refs) - 2) // 2
    fetch(refs[1 : count + 1], refs[count + 1 : -1], refs[-1])


def pack_kernel(*refs):
    sources, out, kept, (prods, grads, taps, sems) = refs[:5], refs[5], refs[6:11], refs[11:]
    fetch(sources, kept, sems)
    keys, values, cotangent, queries, filters = kept
    width = lax.axis_index("width")
    prod = wide(keys[...]) * wide(values[...])
    grad = wide(cotangent[...]) * wide(queries[...])
    for s in range(SUB):
        lanes = slice(LANES * s, LANES * (s + 1))
        prods[pl.ds(s, CTX, stride=SUB), :] = prod[:, lanes]
        grads[pl.ds(s, CTX, stride=SUB), :] = grad[:, lanes]
        taps[pl.ds(s, SUB, stride=SUB), :] = filters[:, lanes]
    own = taps[...]
    words = packed_slots(ORDER_IN)
    for first in range(0, CTX, SUB):
        rows = pl.ds(SUB * first, SUB * SUB)
        pieces = jnp.concatenate([prods[rows, :], grads[rows, :], own], 1)
        pieces = low(pieces_of(pieces))
        for i in range(SUB):
            out[pl.ds(slot_of(words[first + i], width), 1)] = pieces[i : i + 1]


def spread_kernel(arrived, first, second, back, last, twist, spectra, crossing):
    pair = rows_of(wide(arrived[:, :, : 2 * LANES]))
    opened = dot(first[...], low(pair))
    turns = twist[...]
    both = [turned(opened[:, :LANES], turns), turned(opened[:, LANES:], turns)]
    both = dot(jnp.concatenate(both, 0), second[...])
    spectra[...] = low(both)
    prod_real, prod_imag = both[:KEPT, :LANES], both[:KEPT, LANES:]
    grad_real, grad_imag = both[KEPT:, :LANES], both[KEPT:, LANES:]
    real = grad_real * prod_real + grad_imag * prod_imag
    imag = grad_imag * prod_real - grad_real * prod_imag
    opened = dot(low(jnp.concatenate([real, imag], 1)), back[...])
    lag = dot(last[...], reopened(opened, turns))
    lag = lag * (1.0 / (SPAN * math.sqrt(GROUP * LENGTH)))
    crossing[:, :, :LANES] = arrived[:, :, 2 * LANES :]
    crossing[:, :, LANES:] = low(pieces_of(lag))


def filter_kernel(crossed, spectra, first, second, back, last, twist, out):
    turns = twist[...]
    opened = dot(first[...], low(rows_of(wide(crossed[:, :, :LANES]))))
    taps = dot(turned(opened, turns), second[...])
    taps_real, taps_imag = taps[:, :LANES], taps[:, LANES:]
    prod_real, prod_imag = wide(spectra[:KEPT, :LANES]), wide(spectra[:KEPT, LANES:])
    grad_real, grad_imag = wide(spectra[KEPT:, :LANES]), wide(spectra[KEPT:, LANES:])
    real = taps_real * prod_real - taps_imag * prod_imag
    imag = taps_real * prod_imag + taps_imag * prod_real
    response = jnp.concatenate([real, imag], 1)
    real = taps_real * grad_real + taps_imag * grad_imag
    imag = taps_real * grad_imag - taps_imag * grad_real
    pulled = jnp.concatenate([real, imag], 1)
    opened = dot(low(jnp.concatenate([response, pulled], 0)), back[...])
    pair = [reopened(opened[:KEPT], turns), reopened(opened[KEPT:], turns)]
    both = dot(last[...], jnp.concatenate(pair, 1)) * (1.0 / SPAN)
    out[:, :, : 2 * LANES] = low(pieces_of(both))
    out[:, :, 2 * LANES :] = crossed[:, :, LANES:]


def gate_kernel(
    arrived, keys, values, cotangent, queries, mixed, query_grad, key_grad, value_grad, filter_grad, resps, pulls
):
    width = lax.axis_index("width")
    words = packed_slots(ORDER_OUT)
    for first in range(0, CTX, SUB):
        pieces = [arrived[pl.ds(slot_of(words[first + i], width), 1)] for i in range(SUB)]
        pieces = wide(jnp.concatenate(pieces, 0)[:, :, : 2 * LANES]).reshape(SUB * SUB, 2 * LANES)
        rows = pl.ds(SUB * first, SUB * SUB)
        resps[rows, :] = pieces[:, :LANES]
        pulls[rows, :] = pieces[:, LANES:]
    lag = wide(arrived[:, :, 2 * LANES :])
    lag = [sum(lag[k] for k in range(CTX) if ORDER_OUT[k] % SUB == i) for i in range(SUB)]
    for s in range(SUB):
        lanes = slice(LANES * s, LANES * (s + 1))
        response = resps[pl.ds(s, CTX, stride=SUB), :]
        pulled = pulls[pl.ds(s, CTX, stride=SUB), :]
        mixed[:, lanes] = low(wide(queries[:, lanes]) * response)
        query_grad[:, lanes] = low(wide(cotangent[:, lanes]) * response)
        key_grad[:, lanes] = low(pulled * wide(values[:, lanes]))
        value_grad[:, lanes] = low(pulled * wide(keys[:, lanes]))
        filter_grad[:, lanes] = low(jnp.concatenate([part[s : s + 1] for part in lag], 0))


def shape(*dims):
    return jax.ShapeDtypeStruct(dims, jnp.bfloat16)


def call(kernel, out_shape, scratch=(), flops=0, room=24, **kwargs):
    return pl.pallas_call(
        kernel,
        out_shape=out_shape,
        scratch_shapes=scratch,
        cost_estimate=pl.CostEstimate(flops=flops, bytes_accessed=1 << 20, transcendentals=0),
        compiler_params=pltpu.CompilerParams(vmem_limit_bytes=room << 20),
        **kwargs,
    )


def exchange(pieces, order):
    return lax.all_to_all(
        pieces, "ctx", split_axis=0, concat_axis=0, axis_index_groups=[order], tiled=True
    )


def on_device(first, second, back, last, twist, queries, keys, values, cotangent, filters):
    pairs = [(c * 8 + w, partner(c, w)) for c in range(CTX) for w in range(8)]
    channels, local = queries.shape
    def like(array, memory):
        return memory(array.shape, array.dtype)

    anywhere = pl.BlockSpec(memory_space=pl.ANY)
    sources = (keys, values, cotangent, queries, filters)
    packed = call(
        pack_kernel,
        shape(CTX, SUB, 3 * LANES),
        (
            *(like(x, pltpu.VMEM) for x in sources),
            pltpu.VMEM((channels * SUB, LANES), jnp.float32),
            pltpu.VMEM((channels * SUB, LANES), jnp.float32),
            pltpu.VMEM((SUB * SUB, LANES), jnp.float32),
            pltpu.SemaphoreType.DMA((len(sources),)),
        ),
        in_specs=[anywhere] * len(sources),
        room=57,
    )(*sources)
    arrived = exchange(packed, ORDER_IN)
    sources = (first, second, back, last, twist, keys, values, cotangent, queries)
    kept = call(
        keep_kernel,
        tuple(like(x, jax.ShapeDtypeStruct) for x in sources),
        (pltpu.SemaphoreType.DMA((len(sources),)),),
        flops=1_000_000_000,
        in_specs=[anywhere] * (len(sources) + 1),
    )(packed, *sources)
    fixed, gates = kept[:5], kept[5:]
    spectra, crossing = call(
        spread_kernel,
        (shape(2 * KEPT, 2 * LANES), shape(CTX, SUB, 2 * LANES)),
        flops=250_000_000,
    )(arrived, *fixed)
    crossed = lax.ppermute(crossing, AXES, pairs)
    outgoing = call(filter_kernel, shape(CTX, SUB, 3 * LANES), flops=250_000_000)(
        crossed, spectra, *fixed
    )
    returned = exchange(outgoing, ORDER_OUT)
    full = shape(channels, local)
    return call(
        gate_kernel,
        (full, full, full, full, shape(SUB, local)),
        (pltpu.VMEM((channels * SUB, LANES), jnp.float32),) * 2,
    )(returned, *gates)


def solution(mesh):
    spec = P("width", "ctx")
    fixed = tables()
    mapped = jax.shard_map(
        on_device,
        mesh=mesh,
        in_specs=(P(),) * len(fixed) + (spec,) * 5,
        out_specs=(spec,) * 5,
        check_vma=False,
    )

    def run(queries, keys, values, cotangent, filters):
        return mapped(*fixed, queries, keys, values, cotangent, filters)

    return run
```

```python
import math

import jax
import jax.numpy as jnp
import ml_dtypes
import numpy as np
from jax import lax
from jax.experimental import pallas as pl
from jax.experimental.pallas import tpu as pltpu
from jax.sharding import PartitionSpec as P

GROUP = 16
LENGTH = 32768
SPAN = 65536
LANES = 128
COLS = 512
ROWS = LENGTH // LANES
HALF = COLS // 2
EDGE = 16
KEPT = HALF + EDGE
CTX = 64
SUB = 4
AXES = ("ctx", "width")


def shuffled(seed, start):
    order = np.random.RandomState(seed).permutation(CTX).tolist()
    at = order.index(start)
    return order[at:] + order[:at]


PARTNERS = (
    "3e402f9c86db7a15",
    "e125f38d6a9cb704",
    "ae943658720dfb1c",
    "fb84365927d1cae0",
    "ea594268731cbd0f",
    "3f50e28c69ad7b41",
    "bf48259736c0aed1",
    "f125e3d9b7c8a640",
)

ORDER_IN = shuffled(3, 36)
ORDER_OUT = shuffled(9, 36)


def grid_angles(rows, cols, period):
    grid = np.outer(np.arange(rows), np.arange(cols)) % period
    return grid * (2.0 * math.pi / period)


def tables():
    def low(array):
        return np.asarray(array, dtype=np.float32).astype(ml_dtypes.bfloat16)

    grid = grid_angles(HALF + 1, ROWS, COLS)
    first = np.concatenate([np.cos(grid[:HALF]), np.cos(grid[HALF:]), -np.sin(grid[1:HALF])], 0)
    weights = np.full((COLS, 1), 2.0)
    weights[[0, HALF]] = 1.0
    last = low((first * weights).T)
    grid = grid_angles(LANES, LANES, LANES)
    cosine, sine = np.cos(grid), np.sin(grid)
    second = low(np.block([[cosine, -sine], [sine, cosine]]))
    back = low(np.block([[cosine, sine], [-sine, cosine]]))
    grid = grid_angles(HALF + 1, LANES, SPAN)[np.minimum(np.arange(KEPT), HALF)]
    twist = np.concatenate([np.cos(grid), np.sin(grid)], 1).astype(np.float32)
    first, last = low(first)[:, row_order(ORDER_IN)], last[row_order(ORDER_OUT)]
    return first, second, back, last, twist


def dot(left, right):
    return jnp.dot(left, right, preferred_element_type=jnp.float32)


def low(array):
    return array.astype(jnp.bfloat16)


def wide(array):
    return array.astype(jnp.float32)


def rows_of(piece):
    pairs = piece.reshape(CTX // 2, 2, SUB, piece.shape[-1])
    joined = jnp.concatenate([pairs[:, 0], pairs[:, 1]], axis=1)
    return joined.reshape(CTX * SUB, piece.shape[-1])


def pieces_of(rows):
    return rows.reshape(rows.shape[0] // SUB, SUB, rows.shape[1])


def turn(real, imag, twist, sign):
    cosine, sine = twist[:, :LANES], twist[:, LANES:]
    if sign < 0:
        return real * cosine + imag * sine, imag * cosine - real * sine
    return real * cosine - imag * sine, imag * cosine + real * sine


def top_row(shape):
    return lax.broadcasted_iota(jnp.int32, shape, 0) == 0


def turned(opened, twist):
    real, imag = opened[:HALF], opened[HALF:]
    head = imag[:8]
    edge = jnp.broadcast_to(head[:1], (EDGE, LANES))
    head = jnp.where(top_row(head.shape), 0.0, head)
    real = jnp.concatenate([real, edge], 0)
    imag = jnp.concatenate([head, imag[8:], jnp.zeros_like(edge)], 0)
    real, imag = turn(real, imag, twist, -1)
    return low(jnp.concatenate([real, imag], 1))


def reopened(opened, twist):
    real, imag = turn(opened[:, :LANES], opened[:, LANES:], twist, 1)
    head = imag[:8]
    head = jnp.where(top_row(head.shape), real[HALF : HALF + 8], head)
    return low(jnp.concatenate([real[:HALF], head, imag[8:HALF]], 0))


def partner(c, w):
    y, core = 2 * (w // 2) + (c // 8) % 2, w % 2
    other = int(PARTNERS[2 * (c // 16) + (c // 4) % 2][2 * y + core], 16)
    y, core = other // 2, other % 2
    return (c - c % 16 + 8 * (y % 2) + c % 8) * 8 + 2 * (y // 2) + core


def channel(c, w):
    row = partner(c, w) % 8
    half = sum(partner(before, w) % 8 == row for before in range(c % 4, c, 4))
    return 4 * row + c % 4 + 32 * half


def packed_slots(order):
    words = [[0, 0] for _ in range(CTX)]
    for slot, c in enumerate(order):
        for w in range(8):
            words[channel(c, w)][w // 4] |= slot << (8 * (w % 4))
    return words


def slot_of(words, width):
    word = jnp.where(width < 4, jnp.int32(words[0]), jnp.int32(words[1]))
    return jnp.bitwise_and(jnp.right_shift(word, 8 * (width % 4)), 255)


def row_order(order):
    return [SUB * c + s for c in order for s in range(SUB)]


def fetch(sources, targets, sems):
    copies = [
        pltpu.make_async_copy(source, target, sems.at[i])
        for i, (source, target) in enumerate(zip(sources, targets))
    ]
    for copy in copies:
        copy.start()
    for copy in copies:
        copy.wait()


def keep_kernel(*refs):
    count = (len(refs) - 2) // 2
    fetch(refs[1 : count + 1], refs[count + 1 : -1], refs[-1])


def pack_kernel(*refs):
    sources, out, kept, (prods, grads, taps, sems) = refs[:5], refs[5], refs[6:11], refs[11:]
    fetch(sources, kept, sems)
    keys, values, cotangent, queries, filters = kept
    width = lax.axis_index("width")
    prod = wide(keys[...]) * wide(values[...])
    grad = wide(cotangent[...]) * wide(queries[...])
    for s in range(SUB):
        lanes = slice(LANES * s, LANES * (s + 1))
        prods[pl.ds(s, CTX, stride=SUB), :] = prod[:, lanes]
        grads[pl.ds(s, CTX, stride=SUB), :] = grad[:, lanes]
        taps[pl.ds(s, SUB, stride=SUB), :] = filters[:, lanes]
    own = taps[...]
    words = packed_slots(ORDER_IN)
    for first in range(0, CTX, SUB):
        rows = pl.ds(SUB * first, SUB * SUB)
        pieces = jnp.concatenate([prods[rows, :], grads[rows, :], own], 1)
        pieces = low(pieces_of(pieces))
        for i in range(SUB):
            out[pl.ds(slot_of(words[first + i], width), 1)] = pieces[i : i + 1]


def spread_kernel(arrived, first, second, back, last, twist, spectra, crossing):
    pair = rows_of(wide(arrived[:, :, : 2 * LANES]))
    opened = dot(first[...], low(pair))
    turns = twist[...]
    both = [turned(opened[:, :LANES], turns), turned(opened[:, LANES:], turns)]
    both = dot(jnp.concatenate(both, 0), second[...])
    spectra[...] = low(both)
    prod_real, prod_imag = both[:KEPT, :LANES], both[:KEPT, LANES:]
    grad_real, grad_imag = both[KEPT:, :LANES], both[KEPT:, LANES:]
    real = grad_real * prod_real + grad_imag * prod_imag
    imag = grad_imag * prod_real - grad_real * prod_imag
    opened = dot(low(jnp.concatenate([real, imag], 1)), back[...])
    lag = dot(last[...], reopened(opened, turns))
    lag = lag * (1.0 / (SPAN * math.sqrt(GROUP * LENGTH)))
    crossing[:, :, :LANES] = arrived[:, :, 2 * LANES :]
    crossing[:, :, LANES:] = low(pieces_of(lag))


def filter_kernel(crossed, spectra, first, second, back, last, twist, out):
    turns = twist[...]
    opened = dot(first[...], low(rows_of(wide(crossed[:, :, :LANES]))))
    taps = dot(turned(opened, turns), second[...])
    taps_real, taps_imag = taps[:, :LANES], taps[:, LANES:]
    prod_real, prod_imag = wide(spectra[:KEPT, :LANES]), wide(spectra[:KEPT, LANES:])
    grad_real, grad_imag = wide(spectra[KEPT:, :LANES]), wide(spectra[KEPT:, LANES:])
    real = taps_real * prod_real - taps_imag * prod_imag
    imag = taps_real * prod_imag + taps_imag * prod_real
    response = jnp.concatenate([real, imag], 1)
    real = taps_real * grad_real + taps_imag * grad_imag
    imag = taps_real * grad_imag - taps_imag * grad_real
    pulled = jnp.concatenate([real, imag], 1)
    opened = dot(low(jnp.concatenate([response, pulled], 0)), back[...])
    pair = [reopened(opened[:KEPT], turns), reopened(opened[KEPT:], turns)]
    both = dot(last[...], jnp.concatenate(pair, 1)) * (1.0 / SPAN)
    out[:, :, : 2 * LANES] = low(pieces_of(both))
    out[:, :, 2 * LANES :] = crossed[:, :, LANES:]


def gate_kernel(
    arrived, keys, values, cotangent, queries, mixed, query_grad, key_grad, value_grad, filter_grad, resps, pulls
):
    width = lax.axis_index("width")
    words = packed_slots(ORDER_OUT)
    for first in range(0, CTX, SUB):
        pieces = [arrived[pl.ds(slot_of(words[first + i], width), 1)] for i in range(SUB)]
        pieces = wide(jnp.concatenate(pieces, 0)[:, :, : 2 * LANES]).reshape(SUB * SUB, 2 * LANES)
        rows = pl.ds(SUB * first, SUB * SUB)
        resps[rows, :] = pieces[:, :LANES]
        pulls[rows, :] = pieces[:, LANES:]
    lag = wide(arrived[:, :, 2 * LANES :])
    lag = [sum(lag[k] for k in range(CTX) if ORDER_OUT[k] % SUB == i) for i in range(SUB)]
    for s in range(SUB):
        lanes = slice(LANES * s, LANES * (s + 1))
        response = resps[pl.ds(s, CTX, stride=SUB), :]
        pulled = pulls[pl.ds(s, CTX, stride=SUB), :]
        mixed[:, lanes] = low(wide(queries[:, lanes]) * response)
        query_grad[:, lanes] = low(wide(cotangent[:, lanes]) * response)
        key_grad[:, lanes] = low(pulled * wide(values[:, lanes]))
        value_grad[:, lanes] = low(pulled * wide(keys[:, lanes]))
        filter_grad[:, lanes] = low(jnp.concatenate([part[s : s + 1] for part in lag], 0))


def shape(*dims):
    return jax.ShapeDtypeStruct(dims, jnp.bfloat16)


def call(kernel, out_shape, scratch=(), flops=0, room=24, **kwargs):
    return pl.pallas_call(
        kernel,
        out_shape=out_shape,
        scratch_shapes=scratch,
        cost_estimate=pl.CostEstimate(flops=flops, bytes_accessed=1 << 20, transcendentals=0),
        compiler_params=pltpu.CompilerParams(vmem_limit_bytes=room << 20),
        **kwargs,
    )


def exchange(pieces, order):
    return lax.all_to_all(
        pieces, "ctx", split_axis=0, concat_axis=0, axis_index_groups=[order], tiled=True
    )


def on_device(first, second, back, last, twist, queries, keys, values, cotangent, filters):
    pairs = [(c * 8 + w, partner(c, w)) for c in range(CTX) for w in range(8)]
    channels, local = queries.shape
    def like(array, memory):
        return memory(array.shape, array.dtype)

    anywhere = pl.BlockSpec(memory_space=pl.ANY)
    sources = (keys, values, cotangent, queries, filters)
    packed = call(
        pack_kernel,
        shape(CTX, SUB, 3 * LANES),
        (
            *(like(x, pltpu.VMEM) for x in sources),
            pltpu.VMEM((channels * SUB, LANES), jnp.float32),
            pltpu.VMEM((channels * SUB, LANES), jnp.float32),
            pltpu.VMEM((SUB * SUB, LANES), jnp.float32),
            pltpu.SemaphoreType.DMA((len(sources),)),
        ),
        in_specs=[anywhere] * len(sources),
        room=57,
    )(*sources)
    arrived = exchange(packed, ORDER_IN)
    sources = (first, second, back, last, twist, keys, values, cotangent, queries)
    kept = call(
        keep_kernel,
        tuple(like(x, jax.ShapeDtypeStruct) for x in sources),
        (pltpu.SemaphoreType.DMA((len(sources),)),),
        flops=1_000_000_000,
        in_specs=[anywhere] * (len(sources) + 1),
    )(packed, *sources)
    fixed, gates = kept[:5], kept[5:]
    spectra, crossing = call(
        spread_kernel,
        (shape(2 * KEPT, 2 * LANES), shape(CTX, SUB, 2 * LANES)),
        flops=250_000_000,
    )(arrived, *fixed)
    crossed = lax.ppermute(crossing, AXES, pairs)
    outgoing = call(filter_kernel, shape(CTX, SUB, 3 * LANES), flops=250_000_000)(
        crossed, spectra, *fixed
    )
    returned = exchange(outgoing, ORDER_OUT)
    full = shape(channels, local)
    return call(
        gate_kernel,
        (full, full, full, full, shape(SUB, local)),
        (pltpu.VMEM((channels * SUB, LANES), jnp.float32),) * 2,
    )(returned, *gates)


def solution(mesh):
    spec = P("width", "ctx")
    fixed = tables()
    mapped = jax.shard_map(
        on_device,
        mesh=mesh,
        in_specs=(P(),) * len(fixed) + (spec,) * 5,
        out_specs=(spec,) * 5,
        check_vma=False,
    )

    def run(queries, keys, values, cotangent, filters):
        return mapped(*fixed, queries, keys, values, cotangent, filters)

    return run
```

```python
import math

import jax
import jax.numpy as jnp
import ml_dtypes
import numpy as np
from jax import lax
from jax.experimental import pallas as pl
from jax.experimental.pallas import tpu as pltpu
from jax.sharding import PartitionSpec as P

GROUP = 16
LENGTH = 32768
SPAN = 65536
LANES = 128
COLS = 512
ROWS = LENGTH // LANES
HALF = COLS // 2
EDGE = 16
KEPT = HALF + EDGE
CTX = 64
SUB = 4
AXES = ("ctx", "width")


def shuffled(seed, start):
    order = np.random.RandomState(seed).permutation(CTX).tolist()
    at = order.index(start)
    return order[at:] + order[:at]


PARTNERS = (
    "3e402f9c86db7a15",
    "e125f38d6a9cb704",
    "ae943658720dfb1c",
    "fb84365927d1cae0",
    "ea594268731cbd0f",
    "3f50e28c69ad7b41",
    "bf48259736c0aed1",
    "f125e3d9b7c8a640",
)

ORDER_IN = shuffled(3, 36)
ORDER_OUT = shuffled(9, 36)


def grid_angles(rows, cols, period):
    grid = np.outer(np.arange(rows), np.arange(cols)) % period
    return grid * (2.0 * math.pi / period)


def tables():
    def low(array):
        return np.asarray(array, dtype=np.float32).astype(ml_dtypes.bfloat16)

    grid = grid_angles(HALF + 1, ROWS, COLS)
    first = np.concatenate([np.cos(grid[:HALF]), np.cos(grid[HALF:]), -np.sin(grid[1:HALF])], 0)
    weights = np.full((COLS, 1), 2.0)
    weights[[0, HALF]] = 1.0
    last = low((first * weights).T)
    grid = grid_angles(LANES, LANES, LANES)
    cosine, sine = np.cos(grid), np.sin(grid)
    second = low(np.block([[cosine, -sine], [sine, cosine]]))
    back = low(np.block([[cosine, sine], [-sine, cosine]]))
    grid = grid_angles(HALF + 1, LANES, SPAN)[np.minimum(np.arange(KEPT), HALF)]
    twist = np.concatenate([np.cos(grid), np.sin(grid)], 1).astype(np.float32)
    first, last = low(first)[:, row_order(ORDER_IN)], last[row_order(ORDER_OUT)]
    return first, second, back, last, twist


def dot(left, right):
    return jnp.dot(left, right, preferred_element_type=jnp.float32)


def low(array):
    return array.astype(jnp.bfloat16)


def wide(array):
    return array.astype(jnp.float32)


def rows_of(piece):
    pairs = piece.reshape(CTX // 2, 2, SUB, piece.shape[-1])
    joined = jnp.concatenate([pairs[:, 0], pairs[:, 1]], axis=1)
    return joined.reshape(CTX * SUB, piece.shape[-1])


def pieces_of(rows):
    return rows.reshape(rows.shape[0] // SUB, SUB, rows.shape[1])


def turn(real, imag, twist, sign):
    cosine, sine = twist[:, :LANES], twist[:, LANES:]
    if sign < 0:
        return real * cosine + imag * sine, imag * cosine - real * sine
    return real * cosine - imag * sine, imag * cosine + real * sine


def top_row(shape):
    return lax.broadcasted_iota(jnp.int32, shape, 0) == 0


def turned(opened, twist):
    real, imag = opened[:HALF], opened[HALF:]
    head = imag[:8]
    edge = jnp.broadcast_to(head[:1], (EDGE, LANES))
    head = jnp.where(top_row(head.shape), 0.0, head)
    real = jnp.concatenate([real, edge], 0)
    imag = jnp.concatenate([head, imag[8:], jnp.zeros_like(edge)], 0)
    real, imag = turn(real, imag, twist, -1)
    return low(jnp.concatenate([real, imag], 1))


def reopened(opened, twist):
    real, imag = turn(opened[:, :LANES], opened[:, LANES:], twist, 1)
    head = imag[:8]
    head = jnp.where(top_row(head.shape), real[HALF : HALF + 8], head)
    return low(jnp.concatenate([real[:HALF], head, imag[8:HALF]], 0))


def partner(c, w):
    y, core = 2 * (w // 2) + (c // 8) % 2, w % 2
    other = int(PARTNERS[2 * (c // 16) + (c // 4) % 2][2 * y + core], 16)
    y, core = other // 2, other % 2
    return (c - c % 16 + 8 * (y % 2) + c % 8) * 8 + 2 * (y // 2) + core


def channel(c, w):
    row = partner(c, w) % 8
    half = sum(partner(before, w) % 8 == row for before in range(c % 4, c, 4))
    return 4 * row + c % 4 + 32 * half


def packed_slots(order):
    words = [[0, 0] for _ in range(CTX)]
    for slot, c in enumerate(order):
        for w in range(8):
            words[channel(c, w)][w // 4] |= slot << (8 * (w % 4))
    return words


def slot_of(words, width):
    word = jnp.where(width < 4, jnp.int32(words[0]), jnp.int32(words[1]))
    return jnp.bitwise_and(jnp.right_shift(word, 8 * (width % 4)), 255)


def row_order(order):
    return [SUB * c + s for c in order for s in range(SUB)]


def fetch(sources, targets, sems):
    copies = [
        pltpu.make_async_copy(source, target, sems.at[i])
        for i, (source, target) in enumerate(zip(sources, targets))
    ]
    for copy in copies:
        copy.start()
    for copy in copies:
        copy.wait()


def keep_kernel(*refs):
    count = (len(refs) - 2) // 2
    fetch(refs[1 : count + 1], refs[count + 1 : -1], refs[-1])


def pack_kernel(*refs):
    sources, out, kept, (prods, grads, taps, sems) = refs[:5], refs[5], refs[6:11], refs[11:]
    fetch(sources, kept, sems)
    keys, values, cotangent, queries, filters = kept
    width = lax.axis_index("width")
    prod = wide(keys[...]) * wide(values[...])
    grad = wide(cotangent[...]) * wide(queries[...])
    for s in range(SUB):
        lanes = slice(LANES * s, LANES * (s + 1))
        prods[pl.ds(s, CTX, stride=SUB), :] = prod[:, lanes]
        grads[pl.ds(s, CTX, stride=SUB), :] = grad[:, lanes]
        taps[pl.ds(s, SUB, stride=SUB), :] = filters[:, lanes]
    own = taps[...]
    words = packed_slots(ORDER_IN)
    for first in range(0, CTX, SUB):
        rows = pl.ds(SUB * first, SUB * SUB)
        pieces = jnp.concatenate([prods[rows, :], grads[rows, :], own], 1)
        pieces = low(pieces_of(pieces))
        for i in range(SUB):
            out[pl.ds(slot_of(words[first + i], width), 1)] = pieces[i : i + 1]


def spread_kernel(arrived, first, second, back, last, twist, spectra, crossing):
    pair = rows_of(wide(arrived[:, :, : 2 * LANES]))
    opened = dot(first[...], low(pair))
    turns = twist[...]
    both = [turned(opened[:, :LANES], turns), turned(opened[:, LANES:], turns)]
    both = dot(jnp.concatenate(both, 0), second[...])
    spectra[...] = low(both)
    prod_real, prod_imag = both[:KEPT, :LANES], both[:KEPT, LANES:]
    grad_real, grad_imag = both[KEPT:, :LANES], both[KEPT:, LANES:]
    real = grad_real * prod_real + grad_imag * prod_imag
    imag = grad_imag * prod_real - grad_real * prod_imag
    opened = dot(low(jnp.concatenate([real, imag], 1)), back[...])
    lag = dot(last[...], reopened(opened, turns))
    lag = lag * (1.0 / (SPAN * math.sqrt(GROUP * LENGTH)))
    crossing[:, :, :LANES] = arrived[:, :, 2 * LANES :]
    crossing[:, :, LANES:] = low(pieces_of(lag))


def filter_kernel(crossed, spectra, first, second, back, last, twist, out):
    turns = twist[...]
    opened = dot(first[...], low(rows_of(wide(crossed[:, :, :LANES]))))
    taps = dot(turned(opened, turns), second[...])
    taps_real, taps_imag = taps[:, :LANES], taps[:, LANES:]
    prod_real, prod_imag = wide(spectra[:KEPT, :LANES]), wide(spectra[:KEPT, LANES:])
    grad_real, grad_imag = wide(spectra[KEPT:, :LANES]), wide(spectra[KEPT:, LANES:])
    real = taps_real * prod_real - taps_imag * prod_imag
    imag = taps_real * prod_imag + taps_imag * prod_real
    response = jnp.concatenate([real, imag], 1)
    real = taps_real * grad_real + taps_imag * grad_imag
    imag = taps_real * grad_imag - taps_imag * grad_real
    pulled = jnp.concatenate([real, imag], 1)
    opened = dot(low(jnp.concatenate([response, pulled], 0)), back[...])
    pair = [reopened(opened[:KEPT], turns), reopened(opened[KEPT:], turns)]
    both = dot(last[...], jnp.concatenate(pair, 1)) * (1.0 / SPAN)
    out[:, :, : 2 * LANES] = low(pieces_of(both))
    out[:, :, 2 * LANES :] = crossed[:, :, LANES:]


def gate_kernel(arrived, keys, values, cotangent, queries, *refs):
    targets, held, (resps, pulls, sems) = refs[:5], refs[5:10], refs[10:]
    mixed, query_grad, key_grad, value_grad, filter_grad = held
    copies = [pltpu.make_async_copy(held[i], targets[i], sems.at[i]) for i in range(5)]
    width = lax.axis_index("width")
    words = packed_slots(ORDER_OUT)
    for first in range(0, CTX, SUB):
        pieces = [arrived[pl.ds(slot_of(words[first + i], width), 1)] for i in range(SUB)]
        pieces = wide(jnp.concatenate(pieces, 0)[:, :, : 2 * LANES]).reshape(SUB * SUB, 2 * LANES)
        rows = pl.ds(SUB * first, SUB * SUB)
        resps[rows, :] = pieces[:, :LANES]
        pulls[rows, :] = pieces[:, LANES:]
    lag = wide(arrived[:, :, 2 * LANES :])
    lag = [sum(lag[k] for k in range(CTX) if ORDER_OUT[k] % SUB == i) for i in range(SUB)]
    for s in range(SUB):
        lanes = slice(LANES * s, LANES * (s + 1))
        filter_grad[:, lanes] = low(jnp.concatenate([part[s : s + 1] for part in lag], 0))
    copies[4].start()
    for i, (sums, gates) in enumerate(((resps, (queries, cotangent)), (pulls, (values, keys)))):
        for s in range(SUB):
            lanes = slice(LANES * s, LANES * (s + 1))
            part = sums[pl.ds(s, CTX, stride=SUB), :]
            for target, gate in zip(held[2 * i : 2 * i + 2], gates):
                target[:, lanes] = low(part * wide(gate[:, lanes]))
        copies[2 * i].start()
        copies[2 * i + 1].start()
    for copy in copies:
        copy.wait()


def shape(*dims):
    return jax.ShapeDtypeStruct(dims, jnp.bfloat16)


def call(kernel, out_shape, scratch=(), flops=0, room=24, **kwargs):
    return pl.pallas_call(
        kernel,
        out_shape=out_shape,
        scratch_shapes=scratch,
        cost_estimate=pl.CostEstimate(flops=flops, bytes_accessed=1 << 20, transcendentals=0),
        compiler_params=pltpu.CompilerParams(vmem_limit_bytes=room << 20),
        **kwargs,
    )


def exchange(pieces, order):
    return lax.all_to_all(
        pieces, "ctx", split_axis=0, concat_axis=0, axis_index_groups=[order], tiled=True
    )


def on_device(first, second, back, last, twist, queries, keys, values, cotangent, filters):
    pairs = [(c * 8 + w, partner(c, w)) for c in range(CTX) for w in range(8)]
    channels, local = queries.shape
    def like(array, memory):
        return memory(array.shape, array.dtype)

    anywhere = pl.BlockSpec(memory_space=pl.ANY)
    sources = (keys, values, cotangent, queries, filters)
    packed = call(
        pack_kernel,
        shape(CTX, SUB, 3 * LANES),
        (
            *(like(x, pltpu.VMEM) for x in sources),
            pltpu.VMEM((channels * SUB, LANES), jnp.float32),
            pltpu.VMEM((channels * SUB, LANES), jnp.float32),
            pltpu.VMEM((SUB * SUB, LANES), jnp.float32),
            pltpu.SemaphoreType.DMA((len(sources),)),
        ),
        in_specs=[anywhere] * len(sources),
        room=57,
    )(*sources)
    arrived = exchange(packed, ORDER_IN)
    sources = (first, second, back, last, twist, keys, values, cotangent, queries)
    kept = call(
        keep_kernel,
        tuple(like(x, jax.ShapeDtypeStruct) for x in sources),
        (pltpu.SemaphoreType.DMA((len(sources),)),),
        flops=1_000_000_000,
        in_specs=[anywhere] * (len(sources) + 1),
    )(packed, *sources)
    fixed, gates = kept[:5], kept[5:]
    spectra, crossing = call(
        spread_kernel,
        (shape(2 * KEPT, 2 * LANES), shape(CTX, SUB, 2 * LANES)),
        flops=250_000_000,
    )(arrived, *fixed)
    crossed = lax.ppermute(crossing, AXES, pairs)
    outgoing = call(filter_kernel, shape(CTX, SUB, 3 * LANES), flops=250_000_000)(
        crossed, spectra, *fixed
    )
    returned = exchange(outgoing, ORDER_OUT)
    full = shape(channels, local)
    return call(
        gate_kernel,
        (full, full, full, full, shape(SUB, local)),
        (
            *(pltpu.VMEM((channels, local), jnp.bfloat16),) * 4,
            pltpu.VMEM((SUB, local), jnp.bfloat16),
            *(pltpu.VMEM((channels * SUB, LANES), jnp.float32),) * 2,
            pltpu.SemaphoreType.DMA((5,)),
        ),
        out_specs=[anywhere] * 5,
    )(returned, *gates)


def solution(mesh):
    spec = P("width", "ctx")
    fixed = tables()
    mapped = jax.shard_map(
        on_device,
        mesh=mesh,
        in_specs=(P(),) * len(fixed) + (spec,) * 5,
        out_specs=(spec,) * 5,
        check_vma=False,
    )

    def run(queries, keys, values, cotangent, filters):
        return mapped(*fixed, queries, keys, values, cotangent, filters)

    return run
```

```python
import math

import jax
import jax.numpy as jnp
import ml_dtypes
import numpy as np
from jax import lax
from jax.experimental import pallas as pl
from jax.experimental.pallas import tpu as pltpu
from jax.sharding import PartitionSpec as P

GROUP = 16
LENGTH = 32768
SPAN = 65536
LANES = 128
COLS = 512
ROWS = LENGTH // LANES
HALF = COLS // 2
EDGE = 16
KEPT = HALF + EDGE
CTX = 64
SUB = 4
AXES = ("ctx", "width")


def shuffled(seed, start):
    order = np.random.RandomState(seed).permutation(CTX).tolist()
    at = order.index(start)
    return order[at:] + order[:at]


PARTNERS = (
    "3e402f9c86db7a15",
    "e125f38d6a9cb704",
    "ae943658720dfb1c",
    "fb84365927d1cae0",
    "ea594268731cbd0f",
    "3f50e28c69ad7b41",
    "bf48259736c0aed1",
    "f125e3d9b7c8a640",
)

ORDER_IN = shuffled(3, 36)
ORDER_OUT = shuffled(26, 36)


def grid_angles(rows, cols, period):
    grid = np.outer(np.arange(rows), np.arange(cols)) % period
    return grid * (2.0 * math.pi / period)


def tables():
    def low(array):
        return np.asarray(array, dtype=np.float32).astype(ml_dtypes.bfloat16)

    grid = grid_angles(HALF + 1, ROWS, COLS)
    first = np.concatenate([np.cos(grid[:HALF]), np.cos(grid[HALF:]), -np.sin(grid[1:HALF])], 0)
    weights = np.full((COLS, 1), 2.0)
    weights[[0, HALF]] = 1.0
    last = low((first * weights).T)
    grid = grid_angles(LANES, LANES, LANES)
    cosine, sine = np.cos(grid), np.sin(grid)
    second = low(np.block([[cosine, -sine], [sine, cosine]]))
    back = low(np.block([[cosine, sine], [-sine, cosine]]))
    grid = grid_angles(HALF + 1, LANES, SPAN)[np.minimum(np.arange(KEPT), HALF)]
    twist = np.concatenate([np.cos(grid), np.sin(grid)], 1).astype(np.float32)
    first, last = low(first)[:, row_order(ORDER_IN)], last[row_order(ORDER_OUT)]
    return first, second, back, last, twist


def dot(left, right):
    return jnp.dot(left, right, preferred_element_type=jnp.float32)


def low(array):
    return array.astype(jnp.bfloat16)


def wide(array):
    return array.astype(jnp.float32)


def rows_of(piece):
    pairs = piece.reshape(CTX // 2, 2, SUB, piece.shape[-1])
    joined = jnp.concatenate([pairs[:, 0], pairs[:, 1]], axis=1)
    return joined.reshape(CTX * SUB, piece.shape[-1])


def pieces_of(rows):
    return rows.reshape(rows.shape[0] // SUB, SUB, rows.shape[1])


def turn(real, imag, twist, sign):
    cosine, sine = twist[:, :LANES], twist[:, LANES:]
    if sign < 0:
        return real * cosine + imag * sine, imag * cosine - real * sine
    return real * cosine - imag * sine, imag * cosine + real * sine


def top_row(shape):
    return lax.broadcasted_iota(jnp.int32, shape, 0) == 0


def turned(opened, twist):
    real, imag = opened[:HALF], opened[HALF:]
    head = imag[:8]
    edge = jnp.broadcast_to(head[:1], (EDGE, LANES))
    head = jnp.where(top_row(head.shape), 0.0, head)
    real = jnp.concatenate([real, edge], 0)
    imag = jnp.concatenate([head, imag[8:], jnp.zeros_like(edge)], 0)
    real, imag = turn(real, imag, twist, -1)
    return low(jnp.concatenate([real, imag], 1))


def reopened(opened, twist):
    real, imag = turn(opened[:, :LANES], opened[:, LANES:], twist, 1)
    head = imag[:8]
    head = jnp.where(top_row(head.shape), real[HALF : HALF + 8], head)
    return low(jnp.concatenate([real[:HALF], head, imag[8:HALF]], 0))


def partner(c, w):
    y, core = 2 * (w // 2) + (c // 8) % 2, w % 2
    other = int(PARTNERS[2 * (c // 16) + (c // 4) % 2][2 * y + core], 16)
    y, core = other // 2, other % 2
    return (c - c % 16 + 8 * (y % 2) + c % 8) * 8 + 2 * (y // 2) + core


def channel(c, w):
    row = partner(c, w) % 8
    half = sum(partner(before, w) % 8 == row for before in range(c % 4, c, 4))
    return 4 * row + c % 4 + 32 * half


def packed_slots(order):
    words = [[0, 0] for _ in range(CTX)]
    for slot, c in enumerate(order):
        for w in range(8):
            words[channel(c, w)][w // 4] |= slot << (8 * (w % 4))
    return words


def slot_of(words, width):
    word = jnp.where(width < 4, jnp.int32(words[0]), jnp.int32(words[1]))
    return jnp.bitwise_and(jnp.right_shift(word, 8 * (width % 4)), 255)


def row_order(order):
    return [SUB * c + s for c in order for s in range(SUB)]


def fetch(sources, targets, sems):
    copies = [
        pltpu.make_async_copy(source, target, sems.at[i])
        for i, (source, target) in enumerate(zip(sources, targets))
    ]
    for copy in copies:
        copy.start()
    for copy in copies:
        copy.wait()


def keep_kernel(*refs):
    count = (len(refs) - 2) // 2
    fetch(refs[1 : count + 1], refs[count + 1 : -1], refs[-1])


def pack_kernel(*refs):
    sources, out, kept, (prods, grads, taps, sems) = refs[:5], refs[5], refs[6:11], refs[11:]
    fetch(sources, kept, sems)
    keys, values, cotangent, queries, filters = kept
    width = lax.axis_index("width")
    prod = wide(keys[...]) * wide(values[...])
    grad = wide(cotangent[...]) * wide(queries[...])
    for s in range(SUB):
        lanes = slice(LANES * s, LANES * (s + 1))
        prods[pl.ds(s, CTX, stride=SUB), :] = prod[:, lanes]
        grads[pl.ds(s, CTX, stride=SUB), :] = grad[:, lanes]
        taps[pl.ds(s, SUB, stride=SUB), :] = filters[:, lanes]
    own = taps[...]
    words = packed_slots(ORDER_IN)
    for first in range(0, CTX, SUB):
        rows = pl.ds(SUB * first, SUB * SUB)
        pieces = jnp.concatenate([prods[rows, :], grads[rows, :], own], 1)
        pieces = low(pieces_of(pieces))
        for i in range(SUB):
            out[pl.ds(slot_of(words[first + i], width), 1)] = pieces[i : i + 1]


def spread_kernel(arrived, first, second, back, last, twist, spectra, crossing):
    pair = rows_of(wide(arrived[:, :, : 2 * LANES]))
    opened = dot(first[...], low(pair))
    turns = twist[...]
    both = [turned(opened[:, :LANES], turns), turned(opened[:, LANES:], turns)]
    both = dot(jnp.concatenate(both, 0), second[...])
    spectra[...] = low(both)
    prod_real, prod_imag = both[:KEPT, :LANES], both[:KEPT, LANES:]
    grad_real, grad_imag = both[KEPT:, :LANES], both[KEPT:, LANES:]
    real = grad_real * prod_real + grad_imag * prod_imag
    imag = grad_imag * prod_real - grad_real * prod_imag
    opened = dot(low(jnp.concatenate([real, imag], 1)), back[...])
    lag = dot(last[...], reopened(opened, turns))
    lag = lag * (1.0 / (SPAN * math.sqrt(GROUP * LENGTH)))
    crossing[:, :, :LANES] = arrived[:, :, 2 * LANES :]
    crossing[:, :, LANES:] = low(pieces_of(lag))


def filter_kernel(crossed, spectra, first, second, back, last, twist, out):
    turns = twist[...]
    opened = dot(first[...], low(rows_of(wide(crossed[:, :, :LANES]))))
    taps = dot(turned(opened, turns), second[...])
    taps_real, taps_imag = taps[:, :LANES], taps[:, LANES:]
    prod_real, prod_imag = wide(spectra[:KEPT, :LANES]), wide(spectra[:KEPT, LANES:])
    grad_real, grad_imag = wide(spectra[KEPT:, :LANES]), wide(spectra[KEPT:, LANES:])
    real = taps_real * prod_real - taps_imag * prod_imag
    imag = taps_real * prod_imag + taps_imag * prod_real
    response = jnp.concatenate([real, imag], 1)
    real = taps_real * grad_real + taps_imag * grad_imag
    imag = taps_real * grad_imag - taps_imag * grad_real
    pulled = jnp.concatenate([real, imag], 1)
    opened = dot(low(jnp.concatenate([response, pulled], 0)), back[...])
    pair = [reopened(opened[:KEPT], turns), reopened(opened[KEPT:], turns)]
    both = dot(last[...], jnp.concatenate(pair, 1)) * (1.0 / SPAN)
    out[:, :, : 2 * LANES] = low(pieces_of(both))
    out[:, :, 2 * LANES :] = crossed[:, :, LANES:]


def gate_kernel(
    arrived, keys, values, cotangent, queries, mixed, query_grad, key_grad, value_grad, filter_grad, resps, pulls
):
    width = lax.axis_index("width")
    words = packed_slots(ORDER_OUT)
    for first in range(0, CTX, SUB):
        pieces = [arrived[pl.ds(slot_of(words[first + i], width), 1)] for i in range(SUB)]
        pieces = wide(jnp.concatenate(pieces, 0)[:, :, : 2 * LANES]).reshape(SUB * SUB, 2 * LANES)
        rows = pl.ds(SUB * first, SUB * SUB)
        resps[rows, :] = pieces[:, :LANES]
        pulls[rows, :] = pieces[:, LANES:]
    lag = wide(arrived[:, :, 2 * LANES :])
    lag = [sum(lag[k] for k in range(CTX) if ORDER_OUT[k] % SUB == i) for i in range(SUB)]
    for s in range(SUB):
        lanes = slice(LANES * s, LANES * (s + 1))
        response = resps[pl.ds(s, CTX, stride=SUB), :]
        pulled = pulls[pl.ds(s, CTX, stride=SUB), :]
        mixed[:, lanes] = low(wide(queries[:, lanes]) * response)
        query_grad[:, lanes] = low(wide(cotangent[:, lanes]) * response)
        key_grad[:, lanes] = low(pulled * wide(values[:, lanes]))
        value_grad[:, lanes] = low(pulled * wide(keys[:, lanes]))
        filter_grad[:, lanes] = low(jnp.concatenate([part[s : s + 1] for part in lag], 0))


def shape(*dims):
    return jax.ShapeDtypeStruct(dims, jnp.bfloat16)


def call(kernel, out_shape, scratch=(), flops=0, room=24, **kwargs):
    return pl.pallas_call(
        kernel,
        out_shape=out_shape,
        scratch_shapes=scratch,
        cost_estimate=pl.CostEstimate(flops=flops, bytes_accessed=1 << 20, transcendentals=0),
        compiler_params=pltpu.CompilerParams(vmem_limit_bytes=room << 20),
        **kwargs,
    )


def exchange(pieces, order):
    return lax.all_to_all(
        pieces, "ctx", split_axis=0, concat_axis=0, axis_index_groups=[order], tiled=True
    )


def on_device(first, second, back, last, twist, queries, keys, values, cotangent, filters):
    pairs = [(c * 8 + w, partner(c, w)) for c in range(CTX) for w in range(8)]
    channels, local = queries.shape
    def like(array, memory):
        return memory(array.shape, array.dtype)

    anywhere = pl.BlockSpec(memory_space=pl.ANY)
    sources = (keys, values, cotangent, queries, filters)
    packed = call(
        pack_kernel,
        shape(CTX, SUB, 3 * LANES),
        (
            *(like(x, pltpu.VMEM) for x in sources),
            pltpu.VMEM((channels * SUB, LANES), jnp.float32),
            pltpu.VMEM((channels * SUB, LANES), jnp.float32),
            pltpu.VMEM((SUB * SUB, LANES), jnp.float32),
            pltpu.SemaphoreType.DMA((len(sources),)),
        ),
        in_specs=[anywhere] * len(sources),
        room=57,
    )(*sources)
    arrived = exchange(packed, ORDER_IN)
    sources = (first, second, back, last, twist, keys, values, cotangent, queries)
    kept = call(
        keep_kernel,
        tuple(like(x, jax.ShapeDtypeStruct) for x in sources),
        (pltpu.SemaphoreType.DMA((len(sources),)),),
        flops=1_000_000_000,
        in_specs=[anywhere] * (len(sources) + 1),
    )(packed, *sources)
    fixed, gates = kept[:5], kept[5:]
    spectra, crossing = call(
        spread_kernel,
        (shape(2 * KEPT, 2 * LANES), shape(CTX, SUB, 2 * LANES)),
        flops=250_000_000,
    )(arrived, *fixed)
    crossed = lax.ppermute(crossing, AXES, pairs)
    outgoing = call(filter_kernel, shape(CTX, SUB, 3 * LANES), flops=250_000_000)(
        crossed, spectra, *fixed
    )
    returned = exchange(outgoing, ORDER_OUT)
    full = shape(channels, local)
    return call(
        gate_kernel,
        (full, full, full, full, shape(SUB, local)),
        (pltpu.VMEM((channels * SUB, LANES), jnp.float32),) * 2,
    )(returned, *gates)


def solution(mesh):
    spec = P("width", "ctx")
    fixed = tables()
    mapped = jax.shard_map(
        on_device,
        mesh=mesh,
        in_specs=(P(),) * len(fixed) + (spec,) * 5,
        out_specs=(spec,) * 5,
        check_vma=False,
    )

    def run(queries, keys, values, cotangent, filters):
        return mapped(*fixed, queries, keys, values, cotangent, filters)

    return run
```
